32 devices in a mesh: replica: 2 (over y), expert: 4 (over z), tensor: 4 (over x, core).
Axes of the slice: x: 2, y: 2, z: 4, core: 2. Of those that a mesh axis runs over, the one named last changes fastest.
Arguments:
- tokens: bfloat16 [2, 256, 2048], P(None, ('replica', 'expert'), 'tensor'), parts along dimension 1, may hold values from -6 to 6
- expert_ids: int32 [2, 256, 6], P(None, ('replica', 'expert')), parts along dimension 1, may hold values from 0 to 63, all different within a row; in each aligned block of 32 rows (0 to 31, 32 to 63, ..., all dimensions but the last counted through in order) at most 6 rows name the same one
- route_weights: float32 [2, 256, 6], P(None, ('replica', 'expert')), parts along dimension 1, may hold values from 0.05 to 0.5
- w_gate: bfloat16 [64, 2048, 1408], P('expert', None, 'tensor'), may hold values from -0.125 to 0.125
- w_up: bfloat16 [64, 2048, 1408], P('expert', None, 'tensor'), may hold values from -0.125 to 0.125
- w_down: bfloat16 [64, 1408, 2048], P('expert', 'tensor'), may hold values from -0.15625 to 0.15625
Outputs:
- combined: bfloat16 [2, 256, 2048], P(None, ('replica', 'expert'), 'tensor'), parts along dimension 1
The draws below stay inside these ranges and needn't reach their ends.
There are 2 independent parts, one for each index of `replica`. The reference program is written for one: setup_inputs(seed, part) draws one part's arguments, and reference() takes and returns one part's arrays. A program takes and returns all parts, laid end to end along the dimension named above; an argument that names none is the same for every part. Nothing has to cross between parts.
Inputs may be any that keep to these rules, and one draw needn't show every extreme that they name: `expert_ids`: each row names 6 different experts. In each aligned block of 32 rows (the rows of one index of expert at one step) no expert is named by more than 6 rows, a bound that some block reaches.
All inputs are finite; a program needn't handle non-finite values.
Results may differ from the reference program's by a relative error of at most 0.014.
Values may be sent and summed in bfloat16 or wider, within the bound.
No kernel may reach another device: no remote copies, remote signals or barrier semaphores. Data moves between devices by JAX's collectives and lax.ppermute only.
A program may use at most 320 MiB of HBM per device.

```python
import math
import jax
import jax.numpy as jnp
import numpy as np
from jax import lax

D = 2048
FF = 1408
EXPERTS = 64
TOPK = 6
STEPS = 2
TOK_DEV = 32
TOKENS = 128
CAP = 6
N_EXPERT = 4
N_TENSOR = 4


def block_levels(stream_key, shape, pieces, least, high):
    gain = 1.0
    for axis_at, parts in pieces:
        heights = jax.random.uniform(jax.random.fold_in(jax.random.fold_in(stream_key, 6), axis_at), (parts,), jnp.float32, least / len(pieces), high / len(pieces))
        gain = gain * jnp.repeat(jnp.exp(heights), shape[axis_at] // parts).reshape((-1,) + (1,) * (len(shape) - 1 - axis_at))
    return gain


def shared_out(key, own, number, rows, count, top, most, slope):
    sequence = jax.random.permutation(key, count)
    packed, ordinary = shares(count, rows * top, most, slope, True), shares(count, rows * top, most, slope, False)
    places = jnp.arange(count)

    def named(lengths, offset_by):
        used = int((lengths > 0).sum())
        fixed = max(1, used // 4)
        shifted = fixed + (places - fixed + offset_by * (used - fixed)) % max(1, count - fixed)
        return jnp.zeros((count,), jnp.int32).at[sequence[jnp.where(places < fixed, places, shifted)]].set(jnp.asarray(lengths, jnp.int32))

    lengths = jnp.where(number % 4 == 0, named(packed, number // 4), named(ordinary, number - number // 4 - 1))
    mixed = jax.random.permutation(jax.random.fold_in(own, 3), count)
    giver, taker = mixed[0:count // 2 * 2:2], mixed[1:count // 2 * 2:2]
    room = jnp.minimum(lengths[giver] - 1, most - lengths[taker]) // 2
    room = jnp.where((giver == sequence[0]) | (taker == sequence[0]) | (lengths[taker] == 0), 0, jnp.maximum(room, 0))
    shifted = jax.random.randint(jax.random.fold_in(own, 4), (count // 2,), 0, 1 << 20) % (room + 1)
    lengths = lengths.at[giver].add(-shifted).at[taker].add(shifted)
    items = jnp.searchsorted(jnp.cumsum(lengths), jnp.arange(rows * top), side="right").astype(jnp.int32)
    grid = items.reshape(top, rows).T
    grid = grid[jax.random.permutation(jax.random.fold_in(own, 1), rows)]
    offset_by = jax.random.randint(jax.random.fold_in(own, 2), (rows, 1), 0, top)
    return jnp.take_along_axis(grid, (jnp.arange(top)[None, :] + offset_by) % top, axis=1)


def shares(number_of, total, most, slope, full):
    loads = [(1 << 20) // math.isqrt(standing ** slope) + 1 for standing in range(1, number_of + 1)]
    largest = most if full else min(most, max(-(-total // number_of), total * loads[0] // sum(loads)))
    least = 1 if total - largest >= number_of - 1 else 0
    holding, surplus = [largest] + [least] * (number_of - 1), total - largest - least * (number_of - 1)
    while surplus > 0:
        movable = [i for i in range(1, number_of) if holding[i] < largest] or [i for i in range(1, number_of) if holding[i] < most]
        whole, remaining = sum([loads[i] for i in movable]), surplus
        for i in movable:
            extra = min(most - holding[i], max(1, remaining * loads[i] // whole), surplus)
            holding[i] = holding[i] + extra
            surplus = surplus - extra
    return np.array(holding)


def noise(stream_key, extent, deviation, most, split=(), held_as=jnp.bfloat16):
    loudness = block_levels(stream_key, extent, split, -0.22, 0.18) if split else 1.0
    drawn = jax.random.normal(stream_key, extent, jnp.float32) * deviation * loudness
    return jnp.minimum(jnp.maximum(drawn, -most), most).astype(held_as)


def setup_inputs(seed: int = 0, part: int = 0) -> dict:
    arg_keys = jax.random.split(jax.random.key(seed), 7)
    part_keys = jax.random.split(jax.random.fold_in(arg_keys[6], part), 7)
    tokens = noise(part_keys[0], (STEPS, TOKENS, D), 1.0, 6.0, ((1, 4), (2, 4)))
    expert_ids_keys = jax.random.split(jax.random.fold_in(part_keys[1], 1), STEPS * TOKENS // TOK_DEV)
    expert_ids_turns = jax.random.permutation(jax.random.fold_in(part_keys[1], 3), STEPS * TOKENS // TOK_DEV)
    expert_ids = jax.vmap(lambda own, number: shared_out(jax.random.fold_in(part_keys[1], 2), own, number, TOK_DEV, EXPERTS, TOPK, CAP, 2))(expert_ids_keys, expert_ids_turns).reshape((STEPS, TOKENS, TOPK))
    route_weights = jnp.clip(0.05 + 0.45 * jax.random.uniform(part_keys[2], (STEPS, TOKENS, TOPK), jnp.float32) ** block_levels(part_keys[2], (STEPS, TOKENS, TOPK), ((1, 4),), -0.2, 0.2), 0.05, 0.5)
    w_gate = noise(arg_keys[3], (EXPERTS, D, FF), D ** -0.5, 0.125, ((0, 4), (2, 4)))
    w_up = noise(arg_keys[4], (EXPERTS, D, FF), D ** -0.5, 0.125, ((0, 4), (2, 4)))
    w_down = noise(arg_keys[5], (EXPERTS, FF, D), FF ** -0.5, 0.15625, ((0, 4), (1, 4)))
    return dict(tokens=tokens, expert_ids=expert_ids, route_weights=route_weights, w_gate=w_gate, w_up=w_up, w_down=w_down)


def expert_apply(operands):
    inputs, gate_w, up_w, down_w = operands
    gate_val = jnp.dot(inputs, gate_w, preferred_element_type=jnp.float32)
    up_val = jnp.dot(inputs, up_w, preferred_element_type=jnp.float32)
    hidden = (jax.nn.silu(gate_val) * up_val).astype(jnp.bfloat16)
    hidden_blocks = hidden.astype(jnp.float32).reshape(hidden.shape[0], N_TENSOR, FF // N_TENSOR)
    down_blocks = down_w.astype(jnp.float32).reshape(N_TENSOR, FF // N_TENSOR, D)
    partial_output_value = jnp.einsum("rjf,jfd->jrd", hidden_blocks, down_blocks, precision=lax.Precision.HIGHEST)
    partial_output_value = partial_output_value.astype(jnp.bfloat16)
    return jnp.sum(partial_output_value.astype(jnp.float32), axis=0).astype(jnp.bfloat16)


def reference(tokens, expert_ids, route_weights, w_gate, w_up, w_down):
    limit = N_EXPERT * CAP

    def one_step(operands):
        step_tokens, step_ids, step_weights = operands
        flat_ids = step_ids.reshape(TOKENS * TOPK).astype(jnp.int32)
        labels = jnp.arange(EXPERTS, dtype=jnp.int32)
        onehot = (flat_ids[:, None] == labels[None, :]).astype(jnp.int32)
        earlier = (jnp.cumsum(onehot, axis=0) - onehot).astype(jnp.int32)
        position = jnp.sum(earlier * onehot, axis=1).astype(jnp.int32)
        slot_ids = (flat_ids * limit + position).astype(jnp.int32)
        pair_rows = (jnp.arange(TOKENS * TOPK, dtype=jnp.int32) // TOPK).astype(jnp.int32)
        table = jnp.zeros((EXPERTS * limit,), jnp.int32).at[slot_ids].set(pair_rows)
        gathered = step_tokens[table].reshape(EXPERTS, limit, D)
        results = lax.map(expert_apply, (gathered, w_gate, w_up, w_down))
        picked = results.reshape(EXPERTS * limit, D)[slot_ids].reshape(TOKENS, TOPK, D)
        summed = jnp.sum(picked.astype(jnp.float32) * step_weights[:, :, None], axis=1)
        return summed.astype(jnp.bfloat16)

    return lax.map(one_step, (tokens, expert_ids, route_weights))
```

```python
import functools

import jax
import jax.numpy as jnp
from jax import lax
from jax.experimental import pallas as pl
from jax.experimental.pallas import tpu as pltpu
from jax.sharding import PartitionSpec as P

EXPERTS = 64
CAP = 6


def slot_numbers(choice_ids):
    nblocks, nrows, npicks = choice_ids.shape
    flat_ids = choice_ids.reshape(nblocks, nrows * npicks)
    labels = lax.broadcasted_iota(jnp.int32, (1, 1, EXPERTS), 2)
    onehot = (flat_ids[:, :, None] == labels).astype(jnp.int32)
    earlier = jnp.cumsum(onehot, axis=1) - onehot
    position = jnp.sum(earlier * onehot, axis=2)
    return (flat_ids * CAP + position).reshape(nblocks, nrows, npicks)


def dispatch(slot_ids, row_data, slot_total):
    labels = lax.broadcasted_iota(jnp.int32, (1, slot_total, 1, 1), 1)
    chosen = jnp.sum((slot_ids[:, None, :, :] == labels).astype(jnp.int32), axis=3)
    placed = jnp.einsum(
        "bsr,brw->bsw", chosen.astype(jnp.bfloat16), row_data, preferred_element_type=jnp.float32
    )
    return placed.astype(jnp.bfloat16)


def expert_work(arrived_rows, w_gate, w_up, w_down):
    features = lax.all_gather(arrived_rows, "tensor", axis=3, tiled=True)
    decode_step_count, expert_holders, slot_count, feature_width = features.shape
    resident_weights = w_gate.shape[0]
    per_expert = slot_count // resident_weights
    grouped = features.reshape(
        decode_step_count, expert_holders, resident_weights, per_expert, feature_width
    )
    gate_val = jnp.einsum("bhecd,edf->bhecf", grouped, w_gate, preferred_element_type=jnp.float32)
    up_val = jnp.einsum("bhecd,edf->bhecf", grouped, w_up, preferred_element_type=jnp.float32)
    hidden = (jax.nn.silu(gate_val) * up_val).astype(jnp.bfloat16)
    partial_output_value = jnp.einsum(
        "bhecf,efd->bhecd", hidden, w_down, preferred_element_type=jnp.float32
    )
    partial_output_value = partial_output_value.astype(jnp.bfloat16)
    restored = partial_output_value.reshape(
        decode_step_count, expert_holders, slot_count, feature_width
    )
    summed = lax.psum_scatter(
        restored.astype(jnp.float32).astype(jnp.bfloat16), "tensor", scatter_dimension=3, tiled=True
    )
    return lax.all_to_all(summed, "expert", split_axis=1, concat_axis=1, tiled=True)


def per_device(tokens, expert_ids, route_weights, w_gate, w_up, w_down):
    expert_holders = lax.axis_size("expert")
    resident_weights = w_gate.shape[0]
    decode_step_count, nrows, share_width = tokens.shape
    slot_ids = slot_numbers(expert_ids)
    outgoing = dispatch(slot_ids, tokens, EXPERTS * CAP)
    outgoing = outgoing.reshape(
        decode_step_count, expert_holders, resident_weights * CAP, share_width
    )
    returned = expert_work(
        lax.all_to_all(outgoing, "expert", split_axis=1, concat_axis=1, tiled=True),
        w_gate,
        w_up,
        w_down,
    )
    returned = returned.reshape(decode_step_count, EXPERTS * CAP, share_width)
    labels = lax.broadcasted_iota(jnp.int32, (1, 1, 1, EXPERTS * CAP), 3)
    selector = (slot_ids[..., None] == labels).astype(jnp.bfloat16)
    picked = jnp.einsum("brks,bsw->brkw", selector, returned, preferred_element_type=jnp.float32)
    combined = jnp.sum(picked * route_weights[..., None], axis=2)
    return combined.astype(jnp.bfloat16)


NT = (((1,), (1,)), ((), ()))
NN = (((1,), (0,)), ((), ()))
TN = (((0,), (0,)), ((), ()))
META = 128


def dot(a, b, dims):
    return lax.dot_general(a, b, dims, preferred_element_type=jnp.float32)


def route(place, meta, picks, slots, residents, pick_mat, slot_weight):
    rows = meta.shape[0]
    by_pick = meta.astype(jnp.float32).T
    labels = (place[0] + lax.broadcasted_iota(jnp.int32, (residents, rows), 0)).astype(jnp.float32)
    chosen = jnp.zeros((residents, rows), jnp.float32)
    weight = jnp.zeros((residents, rows), jnp.float32)
    for k in range(picks):
        hit = by_pick[k : k + 1, :] == labels
        share = by_pick[picks + k : picks + k + 1, :] + by_pick[2 * picks + k : 2 * picks + k + 1, :]
        chosen = jnp.where(hit, 1.0, chosen)
        weight = jnp.where(hit, share, weight)
    before = lax.broadcasted_iota(jnp.int32, (rows, rows), 0) < lax.broadcasted_iota(jnp.int32, (rows, rows), 1)
    rank = dot(chosen.astype(jnp.bfloat16), before.astype(jnp.bfloat16), NN)
    rank = jnp.where(chosen > 0.0, rank, -1.0)
    numbers = lax.broadcasted_iota(jnp.int32, (slots, rows), 0).astype(jnp.float32)
    for e in range(residents):
        hit = numbers == rank[e : e + 1, :]
        pick_mat[e * slots : (e + 1) * slots, :] = hit.astype(jnp.bfloat16)
        spread = jnp.sum(jnp.where(hit, weight[e : e + 1, :], 0.0), axis=1, keepdims=True)
        slot_weight[e * slots : (e + 1) * slots, :] = jnp.broadcast_to(spread, (slots, 128))


def expert_kernel(picks, slots, place, own, other, meta, wg, wu, wd, out, pick_mat, slot_weight, taken, given):
    e = pl.program_id(0)
    residents = pl.num_programs(0)
    share = own.shape[2]

    def columns(j):
        return pl.ds(pl.multiple_of((place[1] ^ j) * share, share), share)

    @pl.when(e == 0)
    def _():
        route(place, meta[...], picks, slots, pick_mat.shape[0] // slots, pick_mat, slot_weight)
        for j, piece in enumerate((own[0], other[0], own[1], other[1])):
            taken[:, columns(j)] = dot(pick_mat[...], piece, NN).astype(jnp.bfloat16)

    mine = pl.ds(pl.multiple_of(e * slots, slots), slots)
    x = taken[mine, :]
    gate = dot(x, wg[0], NT)
    up = dot(x, wu[0], NT)
    hidden = gate * jax.nn.sigmoid(gate) * up * slot_weight[mine, :1]
    given[mine, :] = dot(hidden.astype(jnp.bfloat16), wd[0], NN).astype(jnp.bfloat16)

    @pl.when(e == residents - 1)
    def _():
        for j in range(4):
            out[j] = dot(pick_mat[...], given[:, columns(j)], TN).astype(jnp.bfloat16)


def experts(place, own, other, meta, wg, wu, wd, picks, slots):
    residents, hidden_units, width = wg.shape
    rows, share = own.shape[1], own.shape[2]
    whole = lambda a: pl.BlockSpec(a.shape, lambda e, *_: (0,) * a.ndim)
    each = lambda a: pl.BlockSpec((1,) + a.shape[1:], lambda e, *_: (e, 0, 0))
    return pl.pallas_call(
        functools.partial(expert_kernel, picks, slots),
        grid_spec=pltpu.PrefetchScalarGridSpec(
            num_scalar_prefetch=1,
            grid=(residents,),
            in_specs=[whole(own), whole(other), whole(meta), each(wg), each(wu), each(wd)],
            out_specs=pl.BlockSpec((4, rows, share), lambda e, *_: (0, 0, 0)),
            scratch_shapes=[
                pltpu.VMEM((residents * slots, rows), jnp.bfloat16),
                pltpu.VMEM((residents * slots, 128), jnp.float32),
                pltpu.VMEM((residents * slots, width), jnp.bfloat16),
                pltpu.VMEM((residents * slots, width), jnp.bfloat16),
            ],
        ),
        out_shape=jax.ShapeDtypeStruct((4, rows, share), jnp.bfloat16),
        compiler_params=pltpu.CompilerParams(vmem_limit_bytes=44 << 20),
    )(place, own, other, meta, wg, wu, wd)


def swap(a, axis, bits):
    n = lax.axis_size(axis)
    return lax.ppermute(a, axis, [(i, i ^ bits) for i in range(n)])


def small_group(tokens, expert_ids, route_weights, w_gate, w_up, w_down):
    steps, nrows, share = tokens.shape
    picks = expert_ids.shape[-1]
    holders = lax.axis_size("expert")
    residents = w_gate.shape[0]
    block = steps * nrows
    slots = steps * holders * CAP
    high = lax.reduce_precision(route_weights, 8, 7)
    meta = jnp.concatenate([expert_ids.astype(jnp.float32), high, route_weights - high], axis=2)
    meta = jnp.pad(meta, ((0, 0), (0, 0), (0, META - 3 * picks))).reshape(block, META).astype(jnp.bfloat16)
    mine = tokens.reshape(block, share)
    pair = jnp.concatenate([mine, swap(mine, "tensor", 2), meta], axis=1)
    held = jnp.stack([pair] + [swap(pair, "expert", k) for k in range(1, holders)])
    held = held.reshape(holders * block, 2 * share + META)
    own = jnp.stack([held[:, :share], held[:, share : 2 * share]])
    other = swap(own, "tensor", 1)
    place = jnp.stack([lax.axis_index("expert") * residents, lax.axis_index("tensor")]).astype(jnp.int32)
    parts = experts(
        place, own, other, held[:, 2 * share :], w_gate.swapaxes(1, 2), w_up.swapaxes(1, 2), w_down, picks, slots
    )
    wide = lambda a: a.astype(jnp.float32)
    came = swap(jnp.stack([parts[1], parts[3]]), "tensor", 1)
    away = (wide(parts[2]) + wide(came[1])).astype(jnp.bfloat16)
    home = wide(parts[0]) + wide(came[0]) + wide(swap(away, "tensor", 2))
    home = home.reshape(holders, block, share)
    sent = home.astype(jnp.bfloat16)
    total = home[0]
    for k in range(1, holders):
        total = total + wide(swap(sent[k], "expert", k))
    return total.reshape(steps, nrows, share).astype(jnp.bfloat16)


def pick_plan(*arrays):
    holders, splits = lax.axis_size("expert"), lax.axis_size("tensor")
    residents = arrays[3].shape[0]
    small = holders == 4 and splits == 4 and residents == 16
    return (small_group if small else per_device)(*arrays)


def solution(mesh):
    return jax.shard_map(
        pick_plan,
        mesh=mesh,
        in_specs=(
            P(None, ("replica", "expert"), "tensor"),
            P(None, ("replica", "expert"), None),
            P(None, ("replica", "expert"), None),
            P("expert", None, "tensor"),
            P("expert", None, "tensor"),
            P("expert", "tensor", None),
        ),
        out_specs=P(None, ("replica", "expert"), "tensor"),
        check_vma=False,
    )
```

```python
import functools

import jax
import jax.numpy as jnp
from jax import lax
from jax.experimental import pallas as pl
from jax.experimental.pallas import tpu as pltpu
from jax.sharding import PartitionSpec as P

EXPERTS = 64
CAP = 6


def slot_numbers(choice_ids):
    nblocks, nrows, npicks = choice_ids.shape
    flat_ids = choice_ids.reshape(nblocks, nrows * npicks)
    labels = lax.broadcasted_iota(jnp.int32, (1, 1, EXPERTS), 2)
    onehot = (flat_ids[:, :, None] == labels).astype(jnp.int32)
    earlier = jnp.cumsum(onehot, axis=1) - onehot
    position = jnp.sum(earlier * onehot, axis=2)
    return (flat_ids * CAP + position).reshape(nblocks, nrows, npicks)


def dispatch(slot_ids, row_data, slot_total):
    labels = lax.broadcasted_iota(jnp.int32, (1, slot_total, 1, 1), 1)
    chosen = jnp.sum((slot_ids[:, None, :, :] == labels).astype(jnp.int32), axis=3)
    placed = jnp.einsum(
        "bsr,brw->bsw", chosen.astype(jnp.bfloat16), row_data, preferred_element_type=jnp.float32
    )
    return placed.astype(jnp.bfloat16)


def expert_work(arrived_rows, w_gate, w_up, w_down):
    features = lax.all_gather(arrived_rows, "tensor", axis=3, tiled=True)
    decode_step_count, expert_holders, slot_count, feature_width = features.shape
    resident_weights = w_gate.shape[0]
    per_expert = slot_count // resident_weights
    grouped = features.reshape(
        decode_step_count, expert_holders, resident_weights, per_expert, feature_width
    )
    gate_val = jnp.einsum("bhecd,edf->bhecf", grouped, w_gate, preferred_element_type=jnp.float32)
    up_val = jnp.einsum("bhecd,edf->bhecf", grouped, w_up, preferred_element_type=jnp.float32)
    hidden = (jax.nn.silu(gate_val) * up_val).astype(jnp.bfloat16)
    partial_output_value = jnp.einsum(
        "bhecf,efd->bhecd", hidden, w_down, preferred_element_type=jnp.float32
    )
    partial_output_value = partial_output_value.astype(jnp.bfloat16)
    restored = partial_output_value.reshape(
        decode_step_count, expert_holders, slot_count, feature_width
    )
    summed = lax.psum_scatter(
        restored.astype(jnp.float32).astype(jnp.bfloat16), "tensor", scatter_dimension=3, tiled=True
    )
    return lax.all_to_all(summed, "expert", split_axis=1, concat_axis=1, tiled=True)


def per_device(tokens, expert_ids, route_weights, w_gate, w_up, w_down):
    expert_holders = lax.axis_size("expert")
    resident_weights = w_gate.shape[0]
    decode_step_count, nrows, share_width = tokens.shape
    slot_ids = slot_numbers(expert_ids)
    outgoing = dispatch(slot_ids, tokens, EXPERTS * CAP)
    outgoing = outgoing.reshape(
        decode_step_count, expert_holders, resident_weights * CAP, share_width
    )
    returned = expert_work(
        lax.all_to_all(outgoing, "expert", split_axis=1, concat_axis=1, tiled=True),
        w_gate,
        w_up,
        w_down,
    )
    returned = returned.reshape(decode_step_count, EXPERTS * CAP, share_width)
    labels = lax.broadcasted_iota(jnp.int32, (1, 1, 1, EXPERTS * CAP), 3)
    selector = (slot_ids[..., None] == labels).astype(jnp.bfloat16)
    picked = jnp.einsum("brks,bsw->brkw", selector, returned, preferred_element_type=jnp.float32)
    combined = jnp.sum(picked * route_weights[..., None], axis=2)
    return combined.astype(jnp.bfloat16)


NT = (((1,), (1,)), ((), ()))
NN = (((1,), (0,)), ((), ()))
TN = (((0,), (0,)), ((), ()))
META = 128
TOPK = 6
GROUP = 2


def dot(a, b, dims):
    return lax.dot_general(a, b, dims, preferred_element_type=jnp.float32)


def route(place, meta, picks, slots, residents, pick_mat, slot_weight):
    rows = meta.shape[0]
    by_pick = meta.astype(jnp.float32).T
    labels = (place[0] + lax.broadcasted_iota(jnp.int32, (residents, rows), 0)).astype(jnp.float32)
    chosen = jnp.zeros((residents, rows), jnp.float32)
    weight = jnp.zeros((residents, rows), jnp.float32)
    for k in range(picks):
        hit = by_pick[k : k + 1, :] == labels
        share = by_pick[picks + k : picks + k + 1, :] + by_pick[2 * picks + k : 2 * picks + k + 1, :]
        chosen = jnp.where(hit, 1.0, chosen)
        weight = jnp.where(hit, share, weight)
    before = lax.broadcasted_iota(jnp.int32, (rows, rows), 0) < lax.broadcasted_iota(jnp.int32, (rows, rows), 1)
    rank = dot(chosen.astype(jnp.bfloat16), before.astype(jnp.bfloat16), NN)
    rank = jnp.where(chosen > 0.0, rank, -1.0)
    numbers = lax.broadcasted_iota(jnp.int32, (slots, rows), 0).astype(jnp.float32)
    for e in range(residents):
        hit = numbers == rank[e : e + 1, :]
        pick_mat[e * slots : (e + 1) * slots, :] = hit.astype(jnp.bfloat16)
        spread = jnp.sum(jnp.where(hit, weight[e : e + 1, :], 0.0), axis=1, keepdims=True)
        slot_weight[e * slots : (e + 1) * slots, :] = jnp.broadcast_to(spread, (slots, 128))


def fetch(weights, buffers, sems, column, e):
    width = buffers[0].shape[2]
    return [
        pltpu.make_async_copy(w.at[e, :, pl.ds(column, width)], b.at[e], sems.at[i, e])
        for i, (w, b) in enumerate(zip(weights, buffers))
    ]


def fetch_all(weights, buffers, sems, column):
    for e in range(buffers[0].shape[0]):
        for copy in fetch(weights, buffers, sems, column, e):
            copy.start()


def place_rows(place, pick_mat, near, far, taken):
    share = near.shape[1]
    low = place[1] & 1
    for column, piece in ((low, near), (1 - low, far)):
        rows = dot(pick_mat[...], piece[...], NN).astype(jnp.bfloat16)
        taken[:, pl.ds(pl.multiple_of(column * share, share), share)] = rows


def add_up(place, pick_back, given, out):
    share = out.shape[2]
    low = place[1] & 1
    for j, column in enumerate((low, 1 - low)):
        block = given[:, pl.ds(pl.multiple_of(column * share, share), share)]
        out[j] = dot(pick_back[...], block, NN).astype(jnp.bfloat16)


def over_experts(residents, slots, work):
    def some(step, carry):
        for g in range(GROUP):
            e = step * GROUP + g
            work(e, pl.ds(pl.multiple_of(e * slots, slots), slots))
        return carry

    lax.fori_loop(0, residents // GROUP, some, 0)


def half_kernel(slots, place, near, far, meta, wg, wu, *rest):
    pick_mat, pick_back, slot_weight, gate, up, taken, bg, bu, sems = rest
    column = pl.multiple_of((place[1] >> 1) * bg.shape[2], bg.shape[2])
    fetch_all((wg, wu), (bg, bu), sems, column)
    route(place, meta[...], TOPK, slots, pick_mat.shape[0] // slots, pick_mat, slot_weight)
    place_rows(place, pick_mat, near, far, taken)
    pick_back[...] = pick_mat[...].T

    def work(e, mine):
        for copy in fetch((wg, wu), (bg, bu), sems, column, e):
            copy.wait()
        x = taken[mine, :]
        gate[mine, :] = dot(x, bg[e], NT)
        up[mine, :] = dot(x, bu[e], NT)

    over_experts(bg.shape[0], slots, work)


def rest_kernel(slots, place, near, far, pick_mat, pick_back, slot_weight, gate, up, wg, wu, wd, *rest):
    hidden, out, taken, given, bg, bu, bd, sems = rest
    column = pl.multiple_of(((place[1] >> 1) ^ 1) * bg.shape[2], bg.shape[2])
    fetch_all((wg, wu, wd), (bg, bu, bd), sems, column)
    place_rows(place, pick_mat, near, far, taken)

    def work(e, mine):
        for copy in fetch((wg, wu, wd), (bg, bu, bd), sems, column, e):
            copy.wait()
        x = taken[mine, :]
        gate_val = gate[mine, :] + dot(x, bg[e], NT)
        up_val = up[mine, :] + dot(x, bu[e], NT)
        scaled = gate_val * jax.nn.sigmoid(gate_val) * up_val * slot_weight[mine, :1]
        scaled = scaled.astype(jnp.bfloat16)
        hidden[mine, :] = scaled
        given[mine, :] = dot(scaled, bd[e], NN).astype(jnp.bfloat16)

    over_experts(bg.shape[0], slots, work)
    add_up(place, pick_back, given, out)


def down_kernel(slots, place, hidden, pick_back, wd, out, given, bd, sems):
    column = pl.multiple_of((place[1] >> 1) * bd.shape[2], bd.shape[2])
    fetch_all((wd,), (bd,), sems, column)

    def work(e, mine):
        for copy in fetch((wd,), (bd,), sems, column, e):
            copy.wait()
        given[mine, :] = dot(hidden[mine, :], bd[e], NN).astype(jnp.bfloat16)

    over_experts(bd.shape[0], slots, work)
    add_up(place, pick_back, given, out)


def call(kernel, args, fetched, outs, scratch, micros):
    vmem, there = pl.BlockSpec(memory_space=pltpu.VMEM), pl.BlockSpec(memory_space=pl.ANY)
    local = len(args) - fetched - 1
    return pl.pallas_call(
        kernel,
        in_specs=[pl.BlockSpec(memory_space=pltpu.SMEM)] + [vmem] * local + [there] * fetched,
        out_specs=jax.tree.map(lambda _: vmem, outs),
        out_shape=outs,
        scratch_shapes=scratch,
        compiler_params=pltpu.CompilerParams(vmem_limit_bytes=48 << 20),
        cost_estimate=pl.CostEstimate(flops=micros * 10**9, bytes_accessed=micros * 3 * 10**6, transcendentals=0),
    )(*args)


def swap(a, axis, bits):
    n = lax.axis_size(axis)
    return lax.ppermute(a, axis, [(i, i ^ bits) for i in range(n)])


def small_group(tokens, expert_ids, route_weights, w_gate, w_up, w_down):
    steps, nrows, share = tokens.shape
    picks = expert_ids.shape[-1]
    holders = lax.axis_size("expert")
    residents = w_gate.shape[0]
    block = steps * nrows
    slots = steps * holders * CAP
    high = lax.reduce_precision(route_weights, 8, 7)
    meta = jnp.concatenate([expert_ids.astype(jnp.float32), high, route_weights - high], axis=2)
    meta = jnp.pad(meta, ((0, 0), (0, 0), (0, META - 3 * picks))).reshape(block, META).astype(jnp.bfloat16)
    mine = jnp.concatenate([tokens.reshape(block, share), meta], axis=1)
    came = {k: swap(mine, "expert", k) for k in (3, 2, 1)}
    held = jnp.concatenate([mine, came[1], came[2], came[3]], axis=0)
    own, meta = held[:, :share], held[:, share:]
    core = swap(own, "tensor", 1)
    across = swap(own, "tensor", 2)
    place = jnp.stack([lax.axis_index("expert") * residents, lax.axis_index("tensor")]).astype(jnp.int32)
    wg, wu, wd = w_gate.swapaxes(1, 2), w_up.swapaxes(1, 2), w_down
    units, width, rows, total = wg.shape[1], wg.shape[2], holders * block, residents * slots
    shape = jax.ShapeDtypeStruct
    pick_mat, pick_back = shape((total, rows), jnp.bfloat16), shape((rows, total), jnp.bfloat16)
    slot_weight, part = shape((total, 128), jnp.float32), shape((total, units), jnp.float32)
    hidden, parts = shape((total, units), jnp.bfloat16), shape((2, rows, share), jnp.bfloat16)
    taken = pltpu.VMEM((total, 2 * share), jnp.bfloat16)
    blocks = pltpu.VMEM((residents, units, 2 * share), jnp.bfloat16)
    sems = lambda n: pltpu.SemaphoreType.DMA((n, residents))
    pick_mat, pick_back, slot_weight, gate, up = call(
        functools.partial(half_kernel, slots),
        (place, own, core, meta, wg, wu),
        2,
        (pick_mat, pick_back, slot_weight, part, part),
        [taken, blocks, blocks, sems(2)],
        9,
    )
    across_late, gate = lax.optimization_barrier((across, gate))
    across_core = swap(across_late, "tensor", 1)
    hidden, away_parts = call(
        functools.partial(rest_kernel, slots),
        (place, across, across_core, pick_mat, pick_back, slot_weight, gate, up, wg, wu, wd),
        3,
        (hidden, parts),
        [taken, taken, blocks, blocks, blocks, sems(3)],
        12,
    )
    wide = lambda a: a.astype(jnp.float32)
    away = (wide(away_parts[0]) + wide(swap(away_parts[1], "tensor", 1))).astype(jnp.bfloat16)
    away, hidden = lax.optimization_barrier((away, hidden))
    back = swap(away, "tensor", 2)
    home_parts = call(
        functools.partial(down_kernel, slots), (place, hidden, pick_back, wd), 1, parts, [taken, blocks, sems(1)], 5
    )
    home_parts, back = lax.optimization_barrier((home_parts, back))
    home = wide(home_parts[0]) + wide(swap(home_parts[1], "tensor", 1)) + wide(back)
    home = home.reshape(holders, block, share)
    sent = home.astype(jnp.bfloat16)
    came = {k: swap(sent[k], "expert", k) for k in (3, 2, 1)}
    result = home[0] + wide(came[1]) + wide(came[2]) + wide(came[3])
    return result.reshape(steps, nrows, share).astype(jnp.bfloat16)


def pick_plan(*arrays):
    holders, splits = lax.axis_size("expert"), lax.axis_size("tensor")
    residents = arrays[3].shape[0]
    small = holders == 4 and splits == 4 and residents == 16
    return (small_group if small else per_device)(*arrays)


def solution(mesh):
    return jax.shard_map(
        pick_plan,
        mesh=mesh,
        in_specs=(
            P(None, ("replica", "expert"), "tensor"),
            P(None, ("replica", "expert"), None),
            P(None, ("replica", "expert"), None),
            P("expert", None, "tensor"),
            P("expert", None, "tensor"),
            P("expert", "tensor", None),
        ),
        out_specs=P(None, ("replica", "expert"), "tensor"),
        check_vma=False,
    )
```

```python
import functools

import jax
import jax.numpy as jnp
from jax import lax
from jax.experimental import pallas as pl
from jax.experimental.pallas import tpu as pltpu
from jax.sharding import PartitionSpec as P

EXPERTS = 64
CAP = 6


def slot_numbers(choice_ids):
    nblocks, nrows, npicks = choice_ids.shape
    flat_ids = choice_ids.reshape(nblocks, nrows * npicks)
    labels = lax.broadcasted_iota(jnp.int32, (1, 1, EXPERTS), 2)
    onehot = (flat_ids[:, :, None] == labels).astype(jnp.int32)
    earlier = jnp.cumsum(onehot, axis=1) - onehot
    position = jnp.sum(earlier * onehot, axis=2)
    return (flat_ids * CAP + position).reshape(nblocks, nrows, npicks)


def dispatch(slot_ids, row_data, slot_total):
    labels = lax.broadcasted_iota(jnp.int32, (1, slot_total, 1, 1), 1)
    chosen = jnp.sum((slot_ids[:, None, :, :] == labels).astype(jnp.int32), axis=3)
    placed = jnp.einsum(
        "bsr,brw->bsw", chosen.astype(jnp.bfloat16), row_data, preferred_element_type=jnp.float32
    )
    return placed.astype(jnp.bfloat16)


def expert_work(arrived_rows, w_gate, w_up, w_down):
    features = lax.all_gather(arrived_rows, "tensor", axis=3, tiled=True)
    decode_step_count, expert_holders, slot_count, feature_width = features.shape
    resident_weights = w_gate.shape[0]
    per_expert = slot_count // resident_weights
    grouped = features.reshape(
        decode_step_count, expert_holders, resident_weights, per_expert, feature_width
    )
    gate_val = jnp.einsum("bhecd,edf->bhecf", grouped, w_gate, preferred_element_type=jnp.float32)
    up_val = jnp.einsum("bhecd,edf->bhecf", grouped, w_up, preferred_element_type=jnp.float32)
    hidden = (jax.nn.silu(gate_val) * up_val).astype(jnp.bfloat16)
    partial_output_value = jnp.einsum(
        "bhecf,efd->bhecd", hidden, w_down, preferred_element_type=jnp.float32
    )
    partial_output_value = partial_output_value.astype(jnp.bfloat16)
    restored = partial_output_value.reshape(
        decode_step_count, expert_holders, slot_count, feature_width
    )
    summed = lax.psum_scatter(
        restored.astype(jnp.float32).astype(jnp.bfloat16), "tensor", scatter_dimension=3, tiled=True
    )
    return lax.all_to_all(summed, "expert", split_axis=1, concat_axis=1, tiled=True)


def per_device(tokens, expert_ids, route_weights, w_gate, w_up, w_down):
    expert_holders = lax.axis_size("expert")
    resident_weights = w_gate.shape[0]
    decode_step_count, nrows, share_width = tokens.shape
    slot_ids = slot_numbers(expert_ids)
    outgoing = dispatch(slot_ids, tokens, EXPERTS * CAP)
    outgoing = outgoing.reshape(
        decode_step_count, expert_holders, resident_weights * CAP, share_width
    )
    returned = expert_work(
        lax.all_to_all(outgoing, "expert", split_axis=1, concat_axis=1, tiled=True),
        w_gate,
        w_up,
        w_down,
    )
    returned = returned.reshape(decode_step_count, EXPERTS * CAP, share_width)
    labels = lax.broadcasted_iota(jnp.int32, (1, 1, 1, EXPERTS * CAP), 3)
    selector = (slot_ids[..., None] == labels).astype(jnp.bfloat16)
    picked = jnp.einsum("brks,bsw->brkw", selector, returned, preferred_element_type=jnp.float32)
    combined = jnp.sum(picked * route_weights[..., None], axis=2)
    return combined.astype(jnp.bfloat16)


NT = (((1,), (1,)), ((), ()))
NN = (((1,), (0,)), ((), ()))
TN = (((0,), (0,)), ((), ()))
TILE = 16
TOPK = 6
GROUP = 4


def dot(a, b, dims):
    return lax.dot_general(a, b, dims, preferred_element_type=jnp.float32)


def pack_kernel(tokens, ids_there, weights_there, out, table, ids, weights, sems):
    nrows = tokens.shape[0]
    copies = [
        pltpu.make_async_copy(ids_there, ids, sems.at[0]),
        pltpu.make_async_copy(weights_there, weights, sems.at[1]),
        pltpu.make_async_copy(tokens, out.at[:nrows], sems.at[2]),
    ]
    for copy in copies:
        copy.start()
    table[...] = jnp.zeros_like(table)
    for copy in copies[:2]:
        copy.wait()
    picks, steps, step_rows = ids.shape
    for s in range(steps):
        high = weights[:, s, :].astype(jnp.bfloat16).astype(jnp.float32)
        low = weights[:, s, :] - high
        for c, part in enumerate((ids[:, s, :].astype(jnp.float32), high, low)):
            table[:picks, c * 128 + s * step_rows : c * 128 + (s + 1) * step_rows] = part
    out[nrows:, :] = table[...].astype(jnp.bfloat16)
    copies[2].wait()


def early_kernel(place, packed, wd, down, sems):
    width = down.shape[2]
    column = pl.multiple_of(((place[1] >> 1) ^ 1) * width, width)
    fetch_all((wd,), (down,), sems, column)
    for e in range(down.shape[0]):
        for copy in fetch((wd,), (down,), sems, column, e):
            copy.wait()


def join_kernel(first, second, third, fourth, out):
    block = out.shape[0] // 4
    for j, piece in enumerate((first, second, third, fourth)):
        out[j * block : (j + 1) * block, :] = piece[:block, :]


def route(place, pieces, picks, slots, residents, table, pick_mat, slot_weight):
    block = pieces[0].shape[0] - TILE
    rows = block * len(pieces)
    for j, piece in enumerate(pieces):
        for c in range(3):
            part = piece[block:, c * 128 : c * 128 + block].astype(jnp.float32)
            table[c * TILE : (c + 1) * TILE, j * block : (j + 1) * block] = part
    labels = (place[0] + lax.broadcasted_iota(jnp.int32, (residents, rows), 0)).astype(jnp.float32)
    chosen = jnp.zeros((residents, rows), jnp.float32)
    weight = jnp.zeros((residents, rows), jnp.float32)
    for k in range(picks):
        hit = table[k : k + 1, :] == labels
        share = table[TILE + k : TILE + k + 1, :] + table[2 * TILE + k : 2 * TILE + k + 1, :]
        chosen = jnp.where(hit, 1.0, chosen)
        weight = jnp.where(hit, share, weight)
    before = lax.broadcasted_iota(jnp.int32, (rows, rows), 0) < lax.broadcasted_iota(jnp.int32, (rows, rows), 1)
    rank = dot(chosen.astype(jnp.bfloat16), before.astype(jnp.bfloat16), NN)
    rank = jnp.where(chosen > 0.0, rank, -1.0)
    numbers = lax.broadcasted_iota(jnp.int32, (slots, rows), 0).astype(jnp.float32)
    for e in range(residents):
        hit = numbers == rank[e : e + 1, :]
        pick_mat[e * slots : (e + 1) * slots, :] = hit.astype(jnp.bfloat16)
        spread = jnp.sum(jnp.where(hit, weight[e : e + 1, :], 0.0), axis=1, keepdims=True)
        slot_weight[e * slots : (e + 1) * slots, :] = jnp.broadcast_to(spread, (slots, 128))


def fetch(weights, buffers, sems, column, e):
    width = buffers[0].shape[2]
    return [
        pltpu.make_async_copy(w.at[e, :, pl.ds(column, width)], b.at[e], sems.at[i, e])
        for i, (w, b) in enumerate(zip(weights, buffers))
    ]


def fetch_all(weights, buffers, sems, column):
    for e in range(buffers[0].shape[0]):
        for copy in fetch(weights, buffers, sems, column, e):
            copy.start()


def place_rows(place, pick_mat, near, far, taken):
    share = near.shape[1]
    low = place[1] & 1
    for column, piece in ((low, near), (1 - low, far)):
        rows = dot(pick_mat[...], piece[...], NN).astype(jnp.bfloat16)
        taken[:, pl.ds(pl.multiple_of(column * share, share), share)] = rows


def add_up(place, pick_back, given, out):
    share = out.shape[2]
    low = place[1] & 1
    for j, column in enumerate((low, 1 - low)):
        block = given[:, pl.ds(pl.multiple_of(column * share, share), share)]
        out[j] = dot(pick_back[...], block, NN).astype(jnp.bfloat16)


def over_experts(residents, slots, arrive, work):
    def some(step, carry):
        group = [step * GROUP + g for g in range(GROUP)]
        for e in group:
            arrive(e)
        work(group, [pl.ds(pl.multiple_of(e * slots, slots), slots) for e in group])
        return carry

    lax.fori_loop(0, residents // GROUP, some, 0)


def half_kernel(slots, place, near, far, one, two, three, four, wg, wu, *rest):
    pick_mat, pick_back, slot_weight, gate, up, taken, table, bg, bu, sems = rest
    width = bg.shape[2]
    column = pl.multiple_of((place[1] >> 1) * width, width)
    residents = bg.shape[0]
    fetch_all((wg, wu), (bg, bu), sems, column)
    route(place, (one, two, three, four), TOPK, slots, residents, table, pick_mat, slot_weight)
    place_rows(place, pick_mat, near, far, taken)
    pick_back[...] = pick_mat[...].T

    def arrive(e):
        for copy in fetch((wg, wu), (bg, bu), sems, column, e):
            copy.wait()

    def work(group, places):
        for e, mine in zip(group, places):
            x = taken[mine, :]
            gate[mine, :] = dot(x, bg[e], NT)
            up[mine, :] = dot(x, bu[e], NT)

    over_experts(residents, slots, arrive, work)


def rest_kernel(slots, place, near, far, pick_mat, pick_back, slot_weight, gate, up, down, wg, wu, *rest):
    hidden, out, taken, given, bg, bu, sems = rest
    column = pl.multiple_of(((place[1] >> 1) ^ 1) * bg.shape[2], bg.shape[2])
    fetch_all((wg, wu), (bg, bu), sems, column)
    place_rows(place, pick_mat, near, far, taken)

    def arrive(e):
        for copy in fetch((wg, wu), (bg, bu), sems, column, e):
            copy.wait()

    def work(group, places):
        ready = []
        for e, mine in zip(group, places):
            x = taken[mine, :]
            gate_val = gate[mine, :] + dot(x, bg[e], NT)
            up_val = up[mine, :] + dot(x, bu[e], NT)
            scaled = gate_val * jax.nn.sigmoid(gate_val) * up_val * slot_weight[mine, :1]
            scaled = scaled.astype(jnp.bfloat16)
            hidden[mine, :] = scaled
            ready.append(scaled)
        for e, mine, scaled in zip(group, places, ready):
            given[mine, :] = dot(scaled, down[e], NN).astype(jnp.bfloat16)

    over_experts(bg.shape[0], slots, arrive, work)
    add_up(place, pick_back, given, out)


def down_kernel(slots, place, hidden, pick_back, wd, out, given, bd, sems):
    column = pl.multiple_of((place[1] >> 1) * bd.shape[2], bd.shape[2])
    fetch_all((wd,), (bd,), sems, column)

    def arrive(e):
        for copy in fetch((wd,), (bd,), sems, column, e):
            copy.wait()

    def work(group, places):
        for e, mine in zip(group, places):
            given[mine, :] = dot(hidden[mine, :], bd[e], NN).astype(jnp.bfloat16)

    over_experts(bd.shape[0], slots, arrive, work)
    add_up(place, pick_back, given, out)


def call(kernel, args, fetched, outs, scratch, micros, room):
    vmem, there = pl.BlockSpec(memory_space=pltpu.VMEM), pl.BlockSpec(memory_space=pl.ANY)
    specs = [vmem if a.ndim > 1 else pl.BlockSpec(memory_space=pltpu.SMEM) for a in args[: len(args) - fetched]]
    return pl.pallas_call(
        kernel,
        in_specs=specs + [there] * fetched,
        out_specs=jax.tree.map(lambda _: vmem, outs),
        out_shape=outs,
        scratch_shapes=scratch,
        compiler_params=pltpu.CompilerParams(vmem_limit_bytes=room << 20),
        cost_estimate=pl.CostEstimate(flops=micros * 10**9, bytes_accessed=micros * 3 * 10**6, transcendentals=0),
    )(*args)


def swap(a, axis, bits):
    n = lax.axis_size(axis)
    return lax.ppermute(a, axis, [(i, i ^ bits) for i in range(n)])


def small_group(tokens, expert_ids, route_weights, w_gate, w_up, w_down):
    steps, nrows, share = tokens.shape
    picks = expert_ids.shape[-1]
    holders = lax.axis_size("expert")
    residents = w_gate.shape[0]
    block = steps * nrows
    slots = steps * holders * CAP
    place = jnp.stack([lax.axis_index("expert") * residents, lax.axis_index("tensor")]).astype(jnp.int32)
    there = lambda a: pltpu.with_memory_space_constraint(a, pltpu.HBM)
    wg, wu, wd = there(w_gate.swapaxes(1, 2)), there(w_up.swapaxes(1, 2)), there(w_down)
    units, rows, total = wg.shape[1], holders * block, residents * slots
    shape = jax.ShapeDtypeStruct
    sources = (tokens.reshape(block, share), expert_ids.transpose(2, 0, 1), route_weights.transpose(2, 0, 1))
    mine = call(
        pack_kernel,
        tuple(there(a) for a in sources),
        3,
        shape((block + TILE, share), jnp.bfloat16),
        [
            pltpu.VMEM((TILE, share), jnp.float32),
            pltpu.VMEM((picks, steps, nrows), jnp.int32),
            pltpu.VMEM((picks, steps, nrows), jnp.float32),
            pltpu.SemaphoreType.DMA((3,)),
        ],
        1,
        2,
    )
    sems = lambda n: pltpu.SemaphoreType.DMA((n, residents))
    down = shape((residents, units, 2 * share), jnp.bfloat16)
    down = call(early_kernel, (place, mine, wd), 1, down, [sems(1)], 5, 2)
    came = {k: swap(mine, "expert", k) for k in (3, 2, 1)}
    pieces, down = lax.optimization_barrier(((mine, came[1], came[2], came[3]), down))
    own = call(join_kernel, pieces, 0, shape((rows, share), jnp.bfloat16), [], 1, 2)
    core = swap(own, "tensor", 1)
    across = swap(own, "tensor", 2)
    pick_mat, pick_back = shape((total, rows), jnp.bfloat16), shape((rows, total), jnp.bfloat16)
    slot_weight, part = shape((total, 128), jnp.float32), shape((total, units), jnp.float32)
    hidden, parts = shape((total, units), jnp.bfloat16), shape((2, rows, share), jnp.bfloat16)
    taken = pltpu.VMEM((total, 2 * share), jnp.bfloat16)
    blocks = pltpu.VMEM(down.shape, jnp.bfloat16)
    pick_mat, pick_back, slot_weight, gate, up = call(
        functools.partial(half_kernel, slots),
        (place, own, core) + pieces + (wg, wu),
        2,
        (pick_mat, pick_back, slot_weight, part, part),
        [taken, pltpu.VMEM((3 * TILE, rows), jnp.float32), blocks, blocks, sems(2)],
        9,
        30,
    )
    across_late, gate = lax.optimization_barrier((across, gate))
    across_core = swap(across_late, "tensor", 1)
    hidden, away_parts = call(
        functools.partial(rest_kernel, slots),
        (place, across, across_core, pick_mat, pick_back, slot_weight, gate, up, down, wg, wu),
        2,
        (hidden, parts),
        [taken, taken, blocks, blocks, sems(2)],
        12,
        32,
    )
    wide = lambda a: a.astype(jnp.float32)
    away = (wide(away_parts[0]) + wide(swap(away_parts[1], "tensor", 1))).astype(jnp.bfloat16)
    away, hidden = lax.optimization_barrier((away, hidden))
    back = swap(away, "tensor", 2)
    home_parts = call(
        functools.partial(down_kernel, slots), (place, hidden, pick_back, wd), 1, parts, [taken, blocks, sems(1)], 5, 44
    )
    home_parts, back = lax.optimization_barrier((home_parts, back))
    home = wide(home_parts[0]) + wide(swap(home_parts[1], "tensor", 1)) + wide(back)
    home = home.reshape(holders, block, share)
    sent = home.astype(jnp.bfloat16)
    came = {k: swap(sent[k], "expert", k) for k in (3, 2, 1)}
    result = home[0] + wide(came[1]) + wide(came[2]) + wide(came[3])
    return result.reshape(steps, nrows, share).astype(jnp.bfloat16)


def pick_plan(*arrays):
    holders, splits = lax.axis_size("expert"), lax.axis_size("tensor")
    residents = arrays[3].shape[0]
    small = holders == 4 and splits == 4 and residents == 16
    return (small_group if small else per_device)(*arrays)


def solution(mesh):
    return jax.shard_map(
        pick_plan,
        mesh=mesh,
        in_specs=(
            P(None, ("replica", "expert"), "tensor"),
            P(None, ("replica", "expert"), None),
            P(None, ("replica", "expert"), None),
            P("expert", None, "tensor"),
            P("expert", None, "tensor"),
            P("expert", "tensor", None),
        ),
        out_specs=P(None, ("replica", "expert"), "tensor"),
        check_vma=False,
    )
```

```python
import functools

import jax
import jax.numpy as jnp
from jax import lax
from jax.experimental import pallas as pl
from jax.experimental.pallas import tpu as pltpu
from jax.sharding import PartitionSpec as P

EXPERTS = 64
CAP = 6


def slot_numbers(choice_ids):
    nblocks, nrows, npicks = choice_ids.shape
    flat_ids = choice_ids.reshape(nblocks, nrows * npicks)
    labels = lax.broadcasted_iota(jnp.int32, (1, 1, EXPERTS), 2)
    onehot = (flat_ids[:, :, None] == labels).astype(jnp.int32)
    earlier = jnp.cumsum(onehot, axis=1) - onehot
    position = jnp.sum(earlier * onehot, axis=2)
    return (flat_ids * CAP + position).reshape(nblocks, nrows, npicks)


def dispatch(slot_ids, row_data, slot_total):
    labels = lax.broadcasted_iota(jnp.int32, (1, slot_total, 1, 1), 1)
    chosen = jnp.sum((slot_ids[:, None, :, :] == labels).astype(jnp.int32), axis=3)
    placed = jnp.einsum(
        "bsr,brw->bsw", chosen.astype(jnp.bfloat16), row_data, preferred_element_type=jnp.float32
    )
    return placed.astype(jnp.bfloat16)


def expert_work(arrived_rows, w_gate, w_up, w_down):
    features = lax.all_gather(arrived_rows, "tensor", axis=3, tiled=True)
    decode_step_count, expert_holders, slot_count, feature_width = features.shape
    resident_weights = w_gate.shape[0]
    per_expert = slot_count // resident_weights
    grouped = features.reshape(
        decode_step_count, expert_holders, resident_weights, per_expert, feature_width
    )
    gate_val = jnp.einsum("bhecd,edf->bhecf", grouped, w_gate, preferred_element_type=jnp.float32)
    up_val = jnp.einsum("bhecd,edf->bhecf", grouped, w_up, preferred_element_type=jnp.float32)
    hidden = (jax.nn.silu(gate_val) * up_val).astype(jnp.bfloat16)
    partial_output_value = jnp.einsum(
        "bhecf,efd->bhecd", hidden, w_down, preferred_element_type=jnp.float32
    )
    partial_output_value = partial_output_value.astype(jnp.bfloat16)
    restored = partial_output_value.reshape(
        decode_step_count, expert_holders, slot_count, feature_width
    )
    summed = lax.psum_scatter(
        restored.astype(jnp.float32).astype(jnp.bfloat16), "tensor", scatter_dimension=3, tiled=True
    )
    return lax.all_to_all(summed, "expert", split_axis=1, concat_axis=1, tiled=True)


def per_device(tokens, expert_ids, route_weights, w_gate, w_up, w_down):
    expert_holders = lax.axis_size("expert")
    resident_weights = w_gate.shape[0]
    decode_step_count, nrows, share_width = tokens.shape
    slot_ids = slot_numbers(expert_ids)
    outgoing = dispatch(slot_ids, tokens, EXPERTS * CAP)
    outgoing = outgoing.reshape(
        decode_step_count, expert_holders, resident_weights * CAP, share_width
    )
    returned = expert_work(
        lax.all_to_all(outgoing, "expert", split_axis=1, concat_axis=1, tiled=True),
        w_gate,
        w_up,
        w_down,
    )
    returned = returned.reshape(decode_step_count, EXPERTS * CAP, share_width)
    labels = lax.broadcasted_iota(jnp.int32, (1, 1, 1, EXPERTS * CAP), 3)
    selector = (slot_ids[..., None] == labels).astype(jnp.bfloat16)
    picked = jnp.einsum("brks,bsw->brkw", selector, returned, preferred_element_type=jnp.float32)
    combined = jnp.sum(picked * route_weights[..., None], axis=2)
    return combined.astype(jnp.bfloat16)


NT = (((1,), (1,)), ((), ()))
NN = (((1,), (0,)), ((), ()))
TN = (((0,), (0,)), ((), ()))
TILE = 16
TOPK = 6
GROUP = 4
FIRST = 4


def dot(a, b, dims):
    return lax.dot_general(a, b, dims, preferred_element_type=jnp.float32)


def pack_kernel(tokens, ids_there, weights_there, out, table, ids, weights, sems):
    nrows = tokens.shape[0]
    copies = [
        pltpu.make_async_copy(ids_there, ids, sems.at[0]),
        pltpu.make_async_copy(weights_there, weights, sems.at[1]),
        pltpu.make_async_copy(tokens, out.at[:nrows], sems.at[2]),
    ]
    for copy in copies:
        copy.start()
    table[...] = jnp.zeros_like(table)
    for copy in copies[:2]:
        copy.wait()
    picks, steps, step_rows = ids.shape
    for s in range(steps):
        high = weights[:, s, :].astype(jnp.bfloat16).astype(jnp.float32)
        low = weights[:, s, :] - high
        for c, part in enumerate((ids[:, s, :].astype(jnp.float32), high, low)):
            table[:picks, c * 128 + s * step_rows : c * 128 + (s + 1) * step_rows] = part
    out[nrows:, :] = table[...].astype(jnp.bfloat16)
    copies[2].wait()


def early_kernel(place, packed, wg, wu, first_g, first_u, sems):
    copies = fetches((wg, wu), (first_g, first_u), sems, near_pair(place, first_g), 0)
    for copy in copies:
        copy.start()
    for copy in copies:
        copy.wait()


def join_kernel(first, second, third, fourth, out):
    block = out.shape[0] // 4
    for j, piece in enumerate((first, second, third, fourth)):
        out[j * block : (j + 1) * block, :] = piece[:block, :]


def route(place, pieces, picks, slots, residents, table, pick_mat, slot_weight):
    block = pieces[0].shape[0] - TILE
    rows = block * len(pieces)
    for j, piece in enumerate(pieces):
        for c in range(3):
            part = piece[block:, c * 128 : c * 128 + block].astype(jnp.float32)
            table[c * TILE : (c + 1) * TILE, j * block : (j + 1) * block] = part
    labels = (place[0] + lax.broadcasted_iota(jnp.int32, (residents, rows), 0)).astype(jnp.float32)
    chosen = jnp.zeros((residents, rows), jnp.float32)
    weight = jnp.zeros((residents, rows), jnp.float32)
    for k in range(picks):
        hit = table[k : k + 1, :] == labels
        share = table[TILE + k : TILE + k + 1, :] + table[2 * TILE + k : 2 * TILE + k + 1, :]
        chosen = jnp.where(hit, 1.0, chosen)
        weight = jnp.where(hit, share, weight)
    before = lax.broadcasted_iota(jnp.int32, (rows, rows), 0) < lax.broadcasted_iota(jnp.int32, (rows, rows), 1)
    rank = dot(chosen.astype(jnp.bfloat16), before.astype(jnp.bfloat16), NN)
    rank = jnp.where(chosen > 0.0, rank, -1.0)
    numbers = lax.broadcasted_iota(jnp.int32, (slots, rows), 0).astype(jnp.float32)
    for e in range(residents):
        hit = numbers == rank[e : e + 1, :]
        pick_mat[e * slots : (e + 1) * slots, :] = hit.astype(jnp.bfloat16)
        spread = jnp.sum(jnp.where(hit, weight[e : e + 1, :], 0.0), axis=1, keepdims=True)
        slot_weight[e * slots : (e + 1) * slots, :] = jnp.broadcast_to(spread, (slots, 128))


def near_pair(place, buffer):
    width = buffer.shape[2]
    return pl.multiple_of((place[1] >> 1) * width, width)


def far_pair(place, buffer):
    width = buffer.shape[2]
    return pl.multiple_of(((place[1] >> 1) ^ 1) * width, width)


def fetches(weights, buffers, sems, column, first, one=None):
    count, _, width = buffers[0].shape
    return [
        pltpu.make_async_copy(w.at[first + e, :, pl.ds(column, width)], b.at[e], sems.at[i, e])
        for e in (range(count) if one is None else (one,))
        for i, (w, b) in enumerate(zip(weights, buffers))
    ]


def wait_all(copies):
    for copy in copies:
        copy.wait()


def place_rows(place, pick_mat, near, far, taken):
    share = near.shape[1]
    low = place[1] & 1
    for column, piece in ((low, near), (1 - low, far)):
        rows = dot(pick_mat[...], piece[...], NN).astype(jnp.bfloat16)
        taken[:, pl.ds(pl.multiple_of(column * share, share), share)] = rows


def add_up(place, pick_back, given, out):
    share = out.shape[2]
    low = place[1] & 1
    for j, column in enumerate((low, 1 - low)):
        block = given[:, pl.ds(pl.multiple_of(column * share, share), share)]
        out[j] = dot(pick_back[...], block, NN).astype(jnp.bfloat16)


def in_groups(first, last, slots, work, after=None, arrive=None, size=2):
    def some(step, carry):
        group = [first + step * size + g for g in range(size)]
        places = [pl.ds(pl.multiple_of(e * slots, slots), slots) for e in group]
        for e in group if arrive else ():
            arrive(e)
        for e, mine in zip(group, places):
            work(e, mine)
        for e, mine in zip(group, places) if after else ():
            after(e, mine)
        return carry

    lax.fori_loop(0, (last - first) // size, some, 0)


def half_kernel(slots, place, near, far, one, two, three, four, first_g, first_u, wg, wu, wd, *rest):
    pick_mat, pick_back, slot_weight, gate, up, down, next_g, next_u, taken, table, bg, bu, sems, ahead = rest
    held = first_g.shape[0]
    residents = held + bg.shape[0]
    later = far_pair(place, bg)
    copies = fetches((wg, wu), (bg, bu), sems, near_pair(place, bg), held)
    early = fetches((wd,), (down,), ahead.at[2:], later, 0) + fetches((wg, wu), (next_g, next_u), ahead, later, 0)
    for copy in copies + early:
        copy.start()
    route(place, (one, two, three, four), TOPK, slots, residents, table, pick_mat, slot_weight)
    place_rows(place, pick_mat, near, far, taken)
    pick_back[...] = pick_mat[...].T

    def work(e, mine, g_block, u_block):
        x = taken[mine, :]
        gate[mine, :] = dot(x, g_block, NT)
        up[mine, :] = dot(x, u_block, NT)

    in_groups(0, held, slots, lambda e, mine: work(e, mine, first_g[e], first_u[e]), size=GROUP)
    wait_all(copies)
    in_groups(held, residents, slots, lambda e, mine: work(e, mine, bg[e - held], bu[e - held]), size=GROUP)
    wait_all(early)


def rest_kernel(slots, place, near, far, pick_mat, pick_back, slot_weight, gate, up, down, next_g, next_u, *rest):
    wg, wu, hidden, out, taken, given, bg, bu, sems = rest
    held = next_g.shape[0]
    residents = held + bg.shape[0]
    copies = fetches((wg, wu), (bg, bu), sems, far_pair(place, bg), held)
    for copy in copies:
        copy.start()
    place_rows(place, pick_mat, near, far, taken)

    def work(e, mine, g_block, u_block):
        x = taken[mine, :]
        gate_val = gate[mine, :] + dot(x, g_block, NT)
        up_val = up[mine, :] + dot(x, u_block, NT)
        scaled = gate_val * jax.nn.sigmoid(gate_val) * up_val * slot_weight[mine, :1]
        hidden[mine, :] = scaled.astype(jnp.bfloat16)

    def lower(e, mine):
        given[mine, :] = dot(hidden[mine, :], down[e], NN).astype(jnp.bfloat16)

    def arrive(e):
        for copy in fetches((wg, wu), (bg, bu), sems, far_pair(place, bg), held, e - held):
            copy.wait()

    in_groups(0, held, slots, lambda e, mine: work(e, mine, next_g[e], next_u[e]), lower)
    in_groups(held, residents, slots, lambda e, mine: work(e, mine, bg[e - held], bu[e - held]), lower, arrive)
    add_up(place, pick_back, given, out)


def down_kernel(slots, place, hidden, pick_back, wd, out, given, bd, sems):
    copies = fetches((wd,), (bd,), sems, near_pair(place, bd), 0)
    for copy in copies:
        copy.start()

    def arrive(e):
        for copy in fetches((wd,), (bd,), sems, near_pair(place, bd), 0, e):
            copy.wait()

    def lower(e, mine):
        given[mine, :] = dot(hidden[mine, :], bd[e], NN).astype(jnp.bfloat16)

    in_groups(0, bd.shape[0], slots, lower, None, arrive)
    add_up(place, pick_back, given, out)


def call(kernel, args, fetched, outs, scratch, micros, room):
    vmem, there = pl.BlockSpec(memory_space=pltpu.VMEM), pl.BlockSpec(memory_space=pl.ANY)
    specs = [vmem if a.ndim > 1 else pl.BlockSpec(memory_space=pltpu.SMEM) for a in args[: len(args) - fetched]]
    return pl.pallas_call(
        kernel,
        in_specs=specs + [there] * fetched,
        out_specs=jax.tree.map(lambda _: vmem, outs),
        out_shape=outs,
        scratch_shapes=scratch,
        compiler_params=pltpu.CompilerParams(vmem_limit_bytes=room << 20),
        cost_estimate=pl.CostEstimate(flops=micros * 10**9, bytes_accessed=micros * 3 * 10**6, transcendentals=0),
    )(*args)


def swap(a, axis, bits):
    n = lax.axis_size(axis)
    return lax.ppermute(a, axis, [(i, i ^ bits) for i in range(n)])


def small_group(tokens, expert_ids, route_weights, w_gate, w_up, w_down):
    steps, nrows, share = tokens.shape
    picks = expert_ids.shape[-1]
    holders = lax.axis_size("expert")
    residents = w_gate.shape[0]
    block = steps * nrows
    slots = steps * holders * CAP
    place = jnp.stack([lax.axis_index("expert") * residents, lax.axis_index("tensor")]).astype(jnp.int32)
    there = lambda a: pltpu.with_memory_space_constraint(a, pltpu.HBM)
    wg, wu, wd = there(w_gate.swapaxes(1, 2)), there(w_up.swapaxes(1, 2)), there(w_down)
    units, rows, total = wg.shape[1], holders * block, residents * slots
    shape = jax.ShapeDtypeStruct
    sources = (tokens.reshape(block, share), expert_ids.transpose(2, 0, 1), route_weights.transpose(2, 0, 1))
    mine = call(
        pack_kernel,
        tuple(there(a) for a in sources),
        3,
        shape((block + TILE, share), jnp.bfloat16),
        [
            pltpu.VMEM((TILE, share), jnp.float32),
            pltpu.VMEM((picks, steps, nrows), jnp.int32),
            pltpu.VMEM((picks, steps, nrows), jnp.float32),
            pltpu.SemaphoreType.DMA((3,)),
        ],
        1,
        2,
    )
    sems = lambda n: pltpu.SemaphoreType.DMA((n, residents))
    several = lambda n: shape((n, units, 2 * share), jnp.bfloat16)
    scratch = lambda n: pltpu.VMEM(several(n).shape, jnp.bfloat16)
    first = residents - FIRST
    first_pair = call(early_kernel, (place, mine, wg, wu), 2, (several(first), several(first)), [sems(2)], 7, 2)
    came = {k: swap(mine, "expert", k) for k in (3, 2, 1)}
    pieces = (mine, came[1], came[2], came[3])
    pieces, first_pair = lax.optimization_barrier((pieces, first_pair))
    own = call(join_kernel, pieces, 0, shape((rows, share), jnp.bfloat16), [], 1, 2)
    core = swap(own, "tensor", 1)
    across = swap(own, "tensor", 2)
    pick_mat, pick_back = shape((total, rows), jnp.bfloat16), shape((rows, total), jnp.bfloat16)
    slot_weight, part = shape((total, 128), jnp.float32), shape((total, units), jnp.float32)
    hidden, parts = shape((total, units), jnp.bfloat16), shape((2, rows, share), jnp.bfloat16)
    taken = pltpu.VMEM((total, 2 * share), jnp.bfloat16)
    pick_mat, pick_back, slot_weight, gate, up, down, *next_pair = call(
        functools.partial(half_kernel, slots),
        (place, own, core) + pieces + tuple(first_pair) + (wg, wu, wd),
        3,
        (pick_mat, pick_back, slot_weight, part, part, several(residents), several(FIRST), several(FIRST)),
        [taken, pltpu.VMEM((3 * TILE, rows), jnp.float32), scratch(FIRST), scratch(FIRST), sems(2), sems(3)],
        9,
        10,
    )
    across_late, gate = lax.optimization_barrier((across, gate))
    across_core = swap(across_late, "tensor", 1)
    hidden, away_parts = call(
        functools.partial(rest_kernel, slots),
        (place, across, across_core, pick_mat, pick_back, slot_weight, gate, up, down, *next_pair, wg, wu),
        2,
        (hidden, parts),
        [taken, taken, scratch(first), scratch(first), sems(2)],
        12,
        24,
    )
    wide = lambda a: a.astype(jnp.float32)
    away = (wide(away_parts[0]) + wide(swap(away_parts[1], "tensor", 1))).astype(jnp.bfloat16)
    away, hidden = lax.optimization_barrier((away, hidden))
    back = swap(away, "tensor", 2)
    home_parts = call(
        functools.partial(down_kernel, slots), (place, hidden, pick_back, wd), 1, parts, [taken, scratch(residents), sems(1)], 5, 16
    )
    home_parts, back = lax.optimization_barrier((home_parts, back))
    home = wide(home_parts[0]) + wide(swap(home_parts[1], "tensor", 1)) + wide(back)
    home = home.reshape(holders, block, share)
    sent = home.astype(jnp.bfloat16)
    came = {k: swap(sent[k], "expert", k) for k in (3, 2, 1)}
    result = home[0] + wide(came[1]) + wide(came[2]) + wide(came[3])
    return result.reshape(steps, nrows, share).astype(jnp.bfloat16)


def pick_plan(*arrays):
    holders, splits = lax.axis_size("expert"), lax.axis_size("tensor")
    residents = arrays[3].shape[0]
    small = holders == 4 and splits == 4 and residents == 16
    return (small_group if small else per_device)(*arrays)


def solution(mesh):
    return jax.shard_map(
        pick_plan,
        mesh=mesh,
        in_specs=(
            P(None, ("replica", "expert"), "tensor"),
            P(None, ("replica", "expert"), None),
            P(None, ("replica", "expert"), None),
            P("expert", None, "tensor"),
            P("expert", None, "tensor"),
            P("expert", "tensor", None),
        ),
        out_specs=P(None, ("replica", "expert"), "tensor"),
        check_vma=False,
    )
```

```python
import functools

import jax
import jax.numpy as jnp
from jax import lax
from jax.experimental import pallas as pl
from jax.experimental.pallas import tpu as pltpu
from jax.sharding import PartitionSpec as P

EXPERTS = 64
CAP = 6


def slot_numbers(choice_ids):
    nblocks, nrows, npicks = choice_ids.shape
    flat_ids = choice_ids.reshape(nblocks, nrows * npicks)
    labels = lax.broadcasted_iota(jnp.int32, (1, 1, EXPERTS), 2)
    onehot = (flat_ids[:, :, None] == labels).astype(jnp.int32)
    earlier = jnp.cumsum(onehot, axis=1) - onehot
    position = jnp.sum(earlier * onehot, axis=2)
    return (flat_ids * CAP + position).reshape(nblocks, nrows, npicks)


def dispatch(slot_ids, row_data, slot_total):
    labels = lax.broadcasted_iota(jnp.int32, (1, slot_total, 1, 1), 1)
    chosen = jnp.sum((slot_ids[:, None, :, :] == labels).astype(jnp.int32), axis=3)
    placed = jnp.einsum(
        "bsr,brw->bsw", chosen.astype(jnp.bfloat16), row_data, preferred_element_type=jnp.float32
    )
    return placed.astype(jnp.bfloat16)


def expert_work(arrived_rows, w_gate, w_up, w_down):
    features = lax.all_gather(arrived_rows, "tensor", axis=3, tiled=True)
    decode_step_count, expert_holders, slot_count, feature_width = features.shape
    resident_weights = w_gate.shape[0]
    per_expert = slot_count // resident_weights
    grouped = features.reshape(
        decode_step_count, expert_holders, resident_weights, per_expert, feature_width
    )
    gate_val = jnp.einsum("bhecd,edf->bhecf", grouped, w_gate, preferred_element_type=jnp.float32)
    up_val = jnp.einsum("bhecd,edf->bhecf", grouped, w_up, preferred_element_type=jnp.float32)
    hidden = (jax.nn.silu(gate_val) * up_val).astype(jnp.bfloat16)
    partial_output_value = jnp.einsum(
        "bhecf,efd->bhecd", hidden, w_down, preferred_element_type=jnp.float32
    )
    partial_output_value = partial_output_value.astype(jnp.bfloat16)
    restored = partial_output_value.reshape(
        decode_step_count, expert_holders, slot_count, feature_width
    )
    summed = lax.psum_scatter(
        restored.astype(jnp.float32).astype(jnp.bfloat16), "tensor", scatter_dimension=3, tiled=True
    )
    return lax.all_to_all(summed, "expert", split_axis=1, concat_axis=1, tiled=True)


def per_device(tokens, expert_ids, route_weights, w_gate, w_up, w_down):
    expert_holders = lax.axis_size("expert")
    resident_weights = w_gate.shape[0]
    decode_step_count, nrows, share_width = tokens.shape
    slot_ids = slot_numbers(expert_ids)
    outgoing = dispatch(slot_ids, tokens, EXPERTS * CAP)
    outgoing = outgoing.reshape(
        decode_step_count, expert_holders, resident_weights * CAP, share_width
    )
    returned = expert_work(
        lax.all_to_all(outgoing, "expert", split_axis=1, concat_axis=1, tiled=True),
        w_gate,
        w_up,
        w_down,
    )
    returned = returned.reshape(decode_step_count, EXPERTS * CAP, share_width)
    labels = lax.broadcasted_iota(jnp.int32, (1, 1, 1, EXPERTS * CAP), 3)
    selector = (slot_ids[..., None] == labels).astype(jnp.bfloat16)
    picked = jnp.einsum("brks,bsw->brkw", selector, returned, preferred_element_type=jnp.float32)
    combined = jnp.sum(picked * route_weights[..., None], axis=2)
    return combined.astype(jnp.bfloat16)


NT = (((1,), (1,)), ((), ()))
NN = (((1,), (0,)), ((), ()))
TN = (((0,), (0,)), ((), ()))
TILE = 16
TOPK = 6
GROUP = 4
FIRST = 4


def dot(a, b, dims):
    return lax.dot_general(a, b, dims, preferred_element_type=jnp.float32)


def pack_kernel(tokens, ids_there, weights_there, out, table, ids, weights, sems):
    share = tokens.shape[1]
    wide = out.shape[1] - table.shape[1]
    copies = [
        pltpu.make_async_copy(ids_there, ids, sems.at[0]),
        pltpu.make_async_copy(weights_there, weights, sems.at[1]),
    ]
    for j in range(wide // share):
        tile = tokens.at[j * TILE : (j + 1) * TILE]
        copies.append(pltpu.make_async_copy(tile, out.at[:, j * share : (j + 1) * share], sems.at[2 + j]))
    for copy in copies:
        copy.start()
    table[...] = jnp.zeros_like(table)
    wait_all(copies[:2])
    picks, steps, step_rows = ids.shape
    half = steps * step_rows
    for s in range(steps):
        high = weights[:, s, :].astype(jnp.bfloat16).astype(jnp.float32)
        low = weights[:, s, :] - high
        at = s * step_rows
        table[:picks, at : at + step_rows] = ids[:, s, :].astype(jnp.float32)
        table[8 : 8 + picks, at : at + step_rows] = high
        table[:picks, half + at : half + at + step_rows] = low
    out[:, wide:] = table[...].astype(jnp.bfloat16)
    wait_all(copies[2:])


def early_kernel(place, packed, wg, wu, first_g, first_u, sems):
    copies = fetches((wg, wu), (first_g, first_u), sems, near_pair(place, first_g), 0)
    for copy in copies:
        copy.start()
    for copy in copies:
        copy.wait()


def join_kernel(first, second, third, fourth, out):
    share = out.shape[1]
    block = out.shape[0] // 4
    for i, piece in enumerate((first, second, third, fourth)):
        for j in range(block // TILE):
            out[i * block + j * TILE : i * block + (j + 1) * TILE, :] = piece[:, j * share : (j + 1) * share]


def route(place, pieces, picks, slots, residents, table, pick_mat, slot_weight):
    rows = table.shape[1]
    block = rows // len(pieces)
    for j, piece in enumerate(pieces):
        packed = piece[:, piece.shape[1] - 2 * block :].astype(jnp.float32)
        here = slice(j * block, (j + 1) * block)
        table[:8, here] = packed[:8, :block]
        table[TILE : TILE + 8, here] = packed[8:, :block]
        table[2 * TILE : 2 * TILE + 8, here] = packed[:8, block:]
    labels = (place[0] + lax.broadcasted_iota(jnp.int32, (residents, rows), 0)).astype(jnp.float32)
    chosen = jnp.zeros((residents, rows), jnp.float32)
    weight = jnp.zeros((residents, rows), jnp.float32)
    for k in range(picks):
        hit = table[k : k + 1, :] == labels
        share = table[TILE + k : TILE + k + 1, :] + table[2 * TILE + k : 2 * TILE + k + 1, :]
        chosen = jnp.where(hit, 1.0, chosen)
        weight = jnp.where(hit, share, weight)
    before = lax.broadcasted_iota(jnp.int32, (rows, rows), 0) < lax.broadcasted_iota(jnp.int32, (rows, rows), 1)
    rank = dot(chosen.astype(jnp.bfloat16), before.astype(jnp.bfloat16), NN)
    rank = jnp.where(chosen > 0.0, rank, -1.0)
    numbers = lax.broadcasted_iota(jnp.int32, (slots, rows), 0).astype(jnp.float32)
    for e in range(residents):
        hit = numbers == rank[e : e + 1, :]
        pick_mat[e * slots : (e + 1) * slots, :] = hit.astype(jnp.bfloat16)
        spread = jnp.sum(jnp.where(hit, weight[e : e + 1, :], 0.0), axis=1, keepdims=True)
        slot_weight[e * slots : (e + 1) * slots, :] = jnp.broadcast_to(spread, (slots, 128))


def near_pair(place, buffer):
    width = buffer.shape[2]
    return pl.multiple_of((place[1] >> 1) * width, width)


def far_pair(place, buffer):
    width = buffer.shape[2]
    return pl.multiple_of(((place[1] >> 1) ^ 1) * width, width)


def fetches(weights, buffers, sems, column, first, one=None):
    count, _, width = buffers[0].shape
    return [
        pltpu.make_async_copy(w.at[first + e, :, pl.ds(column, width)], b.at[e], sems.at[i, e])
        for e in (range(count) if one is None else (one,))
        for i, (w, b) in enumerate(zip(weights, buffers))
    ]


def wait_all(copies):
    for copy in copies:
        copy.wait()


def place_rows(place, pick_mat, near, far, taken):
    share = near.shape[1]
    low = place[1] & 1
    for column, piece in ((low, near), (1 - low, far)):
        rows = dot(pick_mat[...], piece[...], NN).astype(jnp.bfloat16)
        taken[:, pl.ds(pl.multiple_of(column * share, share), share)] = rows


def add_up(place, pick_back, given, out):
    share = out.shape[2]
    low = place[1] & 1
    for j, column in enumerate((low, 1 - low)):
        block = given[:, pl.ds(pl.multiple_of(column * share, share), share)]
        out[j] = dot(pick_back[...], block, NN).astype(jnp.bfloat16)


def in_groups(first, last, slots, work, after=None, arrive=None, size=2):
    def some(step, carry):
        group = [first + step * size + g for g in range(size)]
        places = [pl.ds(pl.multiple_of(e * slots, slots), slots) for e in group]
        for e in group if arrive else ():
            arrive(e)
        for e, mine in zip(group, places):
            work(e, mine)
        for e, mine in zip(group, places) if after else ():
            after(e, mine)
        return carry

    lax.fori_loop(0, (last - first) // size, some, 0)


def half_kernel(slots, place, near, far, one, two, three, four, first_g, first_u, wg, wu, wd, *rest):
    pick_mat, pick_back, slot_weight, gate, up, down, next_g, next_u, taken, table, bg, bu, sems, ahead = rest
    held = first_g.shape[0]
    residents = held + bg.shape[0]
    later = far_pair(place, bg)
    copies = fetches((wg, wu), (bg, bu), sems, near_pair(place, bg), held)
    early = fetches((wd,), (down,), ahead.at[2:], later, 0) + fetches((wg, wu), (next_g, next_u), ahead, later, 0)
    for copy in copies + early:
        copy.start()
    route(place, (one, two, three, four), TOPK, slots, residents, table, pick_mat, slot_weight)
    place_rows(place, pick_mat, near, far, taken)
    pick_back[...] = pick_mat[...].T

    def work(e, mine, g_block, u_block):
        x = taken[mine, :]
        gate[mine, :] = dot(x, g_block, NT)
        up[mine, :] = dot(x, u_block, NT)

    in_groups(0, held, slots, lambda e, mine: work(e, mine, first_g[e], first_u[e]), size=3)
    wait_all(copies)
    in_groups(held, residents, slots, lambda e, mine: work(e, mine, bg[e - held], bu[e - held]), size=GROUP)
    wait_all(early)


def rest_kernel(slots, place, near, far, pick_mat, pick_back, slot_weight, gate, up, down, next_g, next_u, *rest):
    wg, wu, hidden, out, taken, given, bg, bu, sems = rest
    held = next_g.shape[0]
    residents = held + bg.shape[0]
    copies = fetches((wg, wu), (bg, bu), sems, far_pair(place, bg), held)
    for copy in copies:
        copy.start()
    place_rows(place, pick_mat, near, far, taken)

    def work(e, mine, g_block, u_block):
        x = taken[mine, :]
        gate_val = gate[mine, :] + dot(x, g_block, NT)
        up_val = up[mine, :] + dot(x, u_block, NT)
        scaled = gate_val * jax.nn.sigmoid(gate_val) * up_val * slot_weight[mine, :1]
        hidden[mine, :] = scaled.astype(jnp.bfloat16)

    def lower(e, mine):
        given[mine, :] = dot(hidden[mine, :], down[e], NN).astype(jnp.bfloat16)

    def arrive(e):
        for copy in fetches((wg, wu), (bg, bu), sems, far_pair(place, bg), held, e - held):
            copy.wait()

    in_groups(0, held, slots, lambda e, mine: work(e, mine, next_g[e], next_u[e]), lower)
    in_groups(held, residents, slots, lambda e, mine: work(e, mine, bg[e - held], bu[e - held]), lower, arrive, 3)
    add_up(place, pick_back, given, out)


def down_kernel(slots, place, hidden, pick_back, wd, out, given, bd, sems):
    copies = fetches((wd,), (bd,), sems, near_pair(place, bd), 0)
    for copy in copies:
        copy.start()

    def arrive(e):
        for copy in fetches((wd,), (bd,), sems, near_pair(place, bd), 0, e):
            copy.wait()

    def lower(e, mine):
        given[mine, :] = dot(hidden[mine, :], bd[e], NN).astype(jnp.bfloat16)

    in_groups(0, bd.shape[0], slots, lower, None, arrive)
    add_up(place, pick_back, given, out)


def call(kernel, args, fetched, outs, scratch, micros, room):
    vmem, there = pl.BlockSpec(memory_space=pltpu.VMEM), pl.BlockSpec(memory_space=pl.ANY)
    specs = [vmem if a.ndim > 1 else pl.BlockSpec(memory_space=pltpu.SMEM) for a in args[: len(args) - fetched]]
    return pl.pallas_call(
        kernel,
        in_specs=specs + [there] * fetched,
        out_specs=jax.tree.map(lambda _: vmem, outs),
        out_shape=outs,
        scratch_shapes=scratch,
        compiler_params=pltpu.CompilerParams(vmem_limit_bytes=room << 20),
        cost_estimate=pl.CostEstimate(flops=micros * 10**9, bytes_accessed=micros * 3 * 10**6, transcendentals=0),
    )(*args)


def swap(a, axis, bits):
    n = lax.axis_size(axis)
    return lax.ppermute(a, axis, [(i, i ^ bits) for i in range(n)])


def small_group(tokens, expert_ids, route_weights, w_gate, w_up, w_down):
    steps, nrows, share = tokens.shape
    picks = expert_ids.shape[-1]
    holders = lax.axis_size("expert")
    residents = w_gate.shape[0]
    block = steps * nrows
    slots = steps * holders * CAP
    place = jnp.stack([lax.axis_index("expert") * residents, lax.axis_index("tensor")]).astype(jnp.int32)
    there = lambda a: pltpu.with_memory_space_constraint(a, pltpu.HBM)
    wg, wu, wd = there(w_gate.swapaxes(1, 2)), there(w_up.swapaxes(1, 2)), there(w_down)
    units, rows, total = wg.shape[1], holders * block, residents * slots
    shape = jax.ShapeDtypeStruct
    sources = (tokens.reshape(block, share), expert_ids.transpose(2, 0, 1), route_weights.transpose(2, 0, 1))
    mine = call(
        pack_kernel,
        tuple(there(a) for a in sources),
        3,
        shape((TILE, block // TILE * share + 2 * block), jnp.bfloat16),
        [
            pltpu.VMEM((TILE, 2 * block), jnp.float32),
            pltpu.VMEM((picks, steps, nrows), jnp.int32),
            pltpu.VMEM((picks, steps, nrows), jnp.float32),
            pltpu.SemaphoreType.DMA((2 + block // TILE,)),
        ],
        1,
        2,
    )
    sems = lambda n: pltpu.SemaphoreType.DMA((n, residents))
    several = lambda n: shape((n, units, 2 * share), jnp.bfloat16)
    scratch = lambda n: pltpu.VMEM(several(n).shape, jnp.bfloat16)
    first = residents - FIRST
    first_pair = call(early_kernel, (place, mine, wg, wu), 2, (several(first), several(first)), [sems(2)], 7, 2)
    came = {k: swap(mine, "expert", k) for k in (3, 2, 1)}
    pieces = (mine, came[1], came[2], came[3])
    pieces, first_pair = lax.optimization_barrier((pieces, first_pair))
    own = call(join_kernel, pieces, 0, shape((rows, share), jnp.bfloat16), [], 1, 2)
    core = swap(own, "tensor", 1)
    across = swap(own, "tensor", 2)
    pick_mat, pick_back = shape((total, rows), jnp.bfloat16), shape((rows, total), jnp.bfloat16)
    slot_weight, part = shape((total, 128), jnp.float32), shape((total, units), jnp.float32)
    hidden, parts = shape((total, units), jnp.bfloat16), shape((2, rows, share), jnp.bfloat16)
    taken = pltpu.VMEM((total, 2 * share), jnp.bfloat16)
    pick_mat, pick_back, slot_weight, gate, up, down, *next_pair = call(
        functools.partial(half_kernel, slots),
        (place, own, core) + pieces + tuple(first_pair) + (wg, wu, wd),
        3,
        (pick_mat, pick_back, slot_weight, part, part, several(residents), several(FIRST), several(FIRST)),
        [taken, pltpu.VMEM((3 * TILE, rows), jnp.float32), scratch(FIRST), scratch(FIRST), sems(2), sems(3)],
        9,
        10,
    )
    across_late, gate = lax.optimization_barrier((across, gate))
    across_core = swap(across_late, "tensor", 1)
    hidden, away_parts = call(
        functools.partial(rest_kernel, slots),
        (place, across, across_core, pick_mat, pick_back, slot_weight, gate, up, down, *next_pair, wg, wu),
        2,
        (hidden, parts),
        [taken, taken, scratch(first), scratch(first), sems(2)],
        12,
        24,
    )
    wide = lambda a: a.astype(jnp.float32)
    away = (wide(away_parts[0]) + wide(swap(away_parts[1], "tensor", 1))).astype(jnp.bfloat16)
    away, hidden = lax.optimization_barrier((away, hidden))
    back = swap(away, "tensor", 2)
    home_parts = call(
        functools.partial(down_kernel, slots), (place, hidden, pick_back, wd), 1, parts, [taken, scratch(residents), sems(1)], 5, 16
    )
    home_parts, back = lax.optimization_barrier((home_parts, back))
    home = wide(home_parts[0]) + wide(swap(home_parts[1], "tensor", 1)) + wide(back)
    home = home.reshape(holders, block, share)
    sent = home.astype(jnp.bfloat16)
    came = {k: swap(sent[k], "expert", k) for k in (3, 2, 1)}
    result = home[0] + wide(came[1]) + wide(came[2]) + wide(came[3])
    return result.reshape(steps, nrows, share).astype(jnp.bfloat16)


def pick_plan(*arrays):
    holders, splits = lax.axis_size("expert"), lax.axis_size("tensor")
    residents = arrays[3].shape[0]
    block = arrays[0].shape[0] * arrays[0].shape[1]
    small = holders == 4 and splits == 4 and residents == 16 and block == 64
    return (small_group if small else per_device)(*arrays)


def solution(mesh):
    return jax.shard_map(
        pick_plan,
        mesh=mesh,
        in_specs=(
            P(None, ("replica", "expert"), "tensor"),
            P(None, ("replica", "expert"), None),
            P(None, ("replica", "expert"), None),
            P("expert", None, "tensor"),
            P("expert", None, "tensor"),
            P("expert", "tensor", None),
        ),
        out_specs=P(None, ("replica", "expert"), "tensor"),
        check_vma=False,
    )
```

```python
import functools

import jax
import jax.numpy as jnp
from jax import lax
from jax.experimental import pallas as pl
from jax.experimental.pallas import tpu as pltpu
from jax.sharding import PartitionSpec as P

EXPERTS = 64
CAP = 6


def slot_numbers(choice_ids):
    nblocks, nrows, npicks = choice_ids.shape
    flat_ids = choice_ids.reshape(nblocks, nrows * npicks)
    labels = lax.broadcasted_iota(jnp.int32, (1, 1, EXPERTS), 2)
    onehot = (flat_ids[:, :, None] == labels).astype(jnp.int32)
    earlier = jnp.cumsum(onehot, axis=1) - onehot
    position = jnp.sum(earlier * onehot, axis=2)
    return (flat_ids * CAP + position).reshape(nblocks, nrows, npicks)


def dispatch(slot_ids, row_data, slot_total):
    labels = lax.broadcasted_iota(jnp.int32, (1, slot_total, 1, 1), 1)
    chosen = jnp.sum((slot_ids[:, None, :, :] == labels).astype(jnp.int32), axis=3)
    placed = jnp.einsum(
        "bsr,brw->bsw", chosen.astype(jnp.bfloat16), row_data, preferred_element_type=jnp.float32
    )
    return placed.astype(jnp.bfloat16)


def expert_work(arrived_rows, w_gate, w_up, w_down):
    features = lax.all_gather(arrived_rows, "tensor", axis=3, tiled=True)
    decode_step_count, expert_holders, slot_count, feature_width = features.shape
    resident_weights = w_gate.shape[0]
    per_expert = slot_count // resident_weights
    grouped = features.reshape(
        decode_step_count, expert_holders, resident_weights, per_expert, feature_width
    )
    gate_val = jnp.einsum("bhecd,edf->bhecf", grouped, w_gate, preferred_element_type=jnp.float32)
    up_val = jnp.einsum("bhecd,edf->bhecf", grouped, w_up, preferred_element_type=jnp.float32)
    hidden = (jax.nn.silu(gate_val) * up_val).astype(jnp.bfloat16)
    partial_output_value = jnp.einsum(
        "bhecf,efd->bhecd", hidden, w_down, preferred_element_type=jnp.float32
    )
    partial_output_value = partial_output_value.astype(jnp.bfloat16)
    restored = partial_output_value.reshape(
        decode_step_count, expert_holders, slot_count, feature_width
    )
    summed = lax.psum_scatter(
        restored.astype(jnp.float32).astype(jnp.bfloat16), "tensor", scatter_dimension=3, tiled=True
    )
    return lax.all_to_all(summed, "expert", split_axis=1, concat_axis=1, tiled=True)


def per_device(tokens, expert_ids, route_weights, w_gate, w_up, w_down):
    expert_holders = lax.axis_size("expert")
    resident_weights = w_gate.shape[0]
    decode_step_count, nrows, share_width = tokens.shape
    slot_ids = slot_numbers(expert_ids)
    outgoing = dispatch(slot_ids, tokens, EXPERTS * CAP)
    outgoing = outgoing.reshape(
        decode_step_count, expert_holders, resident_weights * CAP, share_width
    )
    returned = expert_work(
        lax.all_to_all(outgoing, "expert", split_axis=1, concat_axis=1, tiled=True),
        w_gate,
        w_up,
        w_down,
    )
    returned = returned.reshape(decode_step_count, EXPERTS * CAP, share_width)
    labels = lax.broadcasted_iota(jnp.int32, (1, 1, 1, EXPERTS * CAP), 3)
    selector = (slot_ids[..., None] == labels).astype(jnp.bfloat16)
    picked = jnp.einsum("brks,bsw->brkw", selector, returned, preferred_element_type=jnp.float32)
    combined = jnp.sum(picked * route_weights[..., None], axis=2)
    return combined.astype(jnp.bfloat16)


NT = (((1,), (1,)), ((), ()))
NN = (((1,), (0,)), ((), ()))
TN = (((0,), (0,)), ((), ()))
TILE = 16
TOPK = 6
GROUP = 4
FIRST = 4


def dot(a, b, dims):
    return lax.dot_general(a, b, dims, preferred_element_type=jnp.float32)


def pack_kernel(tokens, ids_there, weights_there, out, table, ids, weights, sems):
    share = tokens.shape[1]
    wide = out.shape[1] - table.shape[1]
    copies = [
        pltpu.make_async_copy(ids_there, ids, sems.at[0]),
        pltpu.make_async_copy(weights_there, weights, sems.at[1]),
    ]
    for j in range(wide // share):
        tile = tokens.at[j * TILE : (j + 1) * TILE]
        copies.append(pltpu.make_async_copy(tile, out.at[:, j * share : (j + 1) * share], sems.at[2 + j]))
    for copy in copies:
        copy.start()
    table[...] = jnp.zeros_like(table)
    wait_all(copies[:2])
    picks, steps, step_rows = ids.shape
    half = steps * step_rows
    for s in range(steps):
        high = weights[:, s, :].astype(jnp.bfloat16).astype(jnp.float32)
        low = weights[:, s, :] - high
        at = s * step_rows
        table[:picks, at : at + step_rows] = ids[:, s, :].astype(jnp.float32)
        table[8 : 8 + picks, at : at + step_rows] = high
        table[:picks, half + at : half + at + step_rows] = low
    out[:, wide:] = table[...].astype(jnp.bfloat16)
    wait_all(copies[2:])


def early_kernel(place, packed, wg, wu, first_g, first_u, sems):
    copies = fetches((wg, wu), (first_g, first_u), sems, near_pair(place, first_g), 0)
    for copy in copies:
        copy.start()
    for copy in copies:
        copy.wait()


def join_kernel(first, second, third, fourth, out):
    share = out.shape[1]
    block = out.shape[0] // 4
    for i, piece in enumerate((first, second, third, fourth)):
        for j in range(block // TILE):
            out[i * block + j * TILE : i * block + (j + 1) * TILE, :] = piece[:, j * share : (j + 1) * share]


def route(place, pieces, picks, slots, residents, table, pick_mat, slot_weight):
    rows = table.shape[1]
    block = rows // len(pieces)
    for j, piece in enumerate(pieces):
        packed = piece[:, piece.shape[1] - 2 * block :].astype(jnp.float32)
        here = slice(j * block, (j + 1) * block)
        table[:8, here] = packed[:8, :block]
        table[TILE : TILE + 8, here] = packed[8:, :block]
        table[2 * TILE : 2 * TILE + 8, here] = packed[:8, block:]
    labels = (place[0] + lax.broadcasted_iota(jnp.int32, (residents, rows), 0)).astype(jnp.float32)
    chosen = jnp.zeros((residents, rows), jnp.float32)
    weight = jnp.zeros((residents, rows), jnp.float32)
    for k in range(picks):
        hit = table[k : k + 1, :] == labels
        share = table[TILE + k : TILE + k + 1, :] + table[2 * TILE + k : 2 * TILE + k + 1, :]
        chosen = jnp.where(hit, 1.0, chosen)
        weight = jnp.where(hit, share, weight)
    before = lax.broadcasted_iota(jnp.int32, (rows, rows), 0) < lax.broadcasted_iota(jnp.int32, (rows, rows), 1)
    rank = dot(chosen.astype(jnp.bfloat16), before.astype(jnp.bfloat16), NN)
    rank = jnp.where(chosen > 0.0, rank, -1.0)
    numbers = lax.broadcasted_iota(jnp.int32, (slots, rows), 0).astype(jnp.float32)
    for e in range(residents):
        hit = numbers == rank[e : e + 1, :]
        pick_mat[e * slots : (e + 1) * slots, :] = hit.astype(jnp.bfloat16)
        spread = jnp.sum(jnp.where(hit, weight[e : e + 1, :], 0.0), axis=1, keepdims=True)
        slot_weight[e * slots : (e + 1) * slots, :] = jnp.broadcast_to(spread, (slots, 128))


def near_pair(place, buffer):
    width = buffer.shape[2]
    return pl.multiple_of((place[1] >> 1) * width, width)


def far_pair(place, buffer):
    width = buffer.shape[2]
    return pl.multiple_of(((place[1] >> 1) ^ 1) * width, width)


def fetches(weights, buffers, sems, column, first, one=None):
    count, _, width = buffers[0].shape
    return [
        pltpu.make_async_copy(w.at[first + e, :, pl.ds(column, width)], b.at[e], sems.at[i, e])
        for e in (range(count) if one is None else (one,))
        for i, (w, b) in enumerate(zip(weights, buffers))
    ]


def wait_all(copies):
    for copy in copies:
        copy.wait()


def place_rows(place, pick_mat, near, far, taken):
    share = near.shape[1]
    low = place[1] & 1
    for column, piece in ((low, near), (1 - low, far)):
        rows = dot(pick_mat[...], piece[...], NN).astype(jnp.bfloat16)
        taken[:, pl.ds(pl.multiple_of(column * share, share), share)] = rows


def in_groups(first, last, slots, work, after=None, arrive=None, size=2):
    def some(step, carry):
        group = [first + step * size + g for g in range(size)]
        places = [pl.ds(pl.multiple_of(e * slots, slots), slots) for e in group]
        for e in group if arrive else ():
            arrive(e)
        for e, mine in zip(group, places):
            work(e, mine)
        for e, mine in zip(group, places) if after else ():
            after(e, mine)
        return carry

    lax.fori_loop(0, (last - first) // size, some, 0)


def half_kernel(slots, place, near, far, one, two, three, four, first_g, first_u, wg, wu, wd, *rest):
    pick_mat, pick_back, slot_weight, gate, up, down, next_g, next_u, taken, table, bg, bu, sems, ahead = rest
    held = first_g.shape[0]
    residents = held + bg.shape[0]
    later = far_pair(place, bg)
    copies = fetches((wg, wu), (bg, bu), sems, near_pair(place, bg), held)
    share = near.shape[1]
    early = [
        pltpu.make_async_copy(
            wd.at[e, :, pl.ds(pl.multiple_of((place[1] ^ (3 - 2 * j)) * share, share), share)],
            down.at[e, :, j * share : (j + 1) * share],
            ahead.at[2 + j, e],
        )
        for e in range(residents)
        for j in range(2)
    ]
    early = early + fetches((wg, wu), (next_g, next_u), ahead, later, 0)
    for copy in copies + early:
        copy.start()
    route(place, (one, two, three, four), TOPK, slots, residents, table, pick_mat, slot_weight)
    place_rows(place, pick_mat, near, far, taken)
    pick_back[...] = pick_mat[...].T

    def work(e, mine, g_block, u_block):
        x = taken[mine, :]
        gate[mine, :] = dot(x, g_block, NT)
        up[mine, :] = dot(x, u_block, NT)

    in_groups(0, held, slots, lambda e, mine: work(e, mine, first_g[e], first_u[e]), size=3)
    wait_all(copies)
    in_groups(held, residents, slots, lambda e, mine: work(e, mine, bg[e - held], bu[e - held]), size=GROUP)
    wait_all(early)


def rest_kernel(slots, place, near, far, pick_mat, pick_back, slot_weight, gate, up, down, next_g, next_u, *rest):
    wg, wu, wd, hidden, out, away_down, taken, given, bg, bu, sems, ahead = rest
    held = next_g.shape[0]
    residents = held + bg.shape[0]
    share = out.shape[2]
    away_columns = pl.multiple_of((place[1] ^ 2) * share, share)
    early = fetches((wd,), (away_down,), ahead, away_columns, 0)
    for copy in fetches((wg, wu), (bg, bu), sems, far_pair(place, bg), held) + early:
        copy.start()
    place_rows(place, pick_mat, near, far, taken)

    def work(e, mine, g_block, u_block):
        x = taken[mine, :]
        gate_val = gate[mine, :] + dot(x, g_block, NT)
        up_val = up[mine, :] + dot(x, u_block, NT)
        scaled = gate_val * jax.nn.sigmoid(gate_val) * up_val * slot_weight[mine, :1]
        hidden[mine, :] = scaled.astype(jnp.bfloat16)

    def lower(e, mine):
        given[mine, :] = dot(hidden[mine, :], down[e], NN).astype(jnp.bfloat16)

    def arrive(e):
        wait_all(fetches((wg, wu), (bg, bu), sems, far_pair(place, bg), held, e - held))

    in_groups(0, held, slots, lambda e, mine: work(e, mine, next_g[e], next_u[e]), lower)
    in_groups(held, residents, slots, lambda e, mine: work(e, mine, bg[e - held], bu[e - held]), lower, arrive, 3)
    wait_all(early)
    for j in range(2):
        out[j] = dot(pick_back[...], given[:, j * share : (j + 1) * share], NN).astype(jnp.bfloat16)


def lower_kernel(slots, place, hidden, pick_back, down, out, given):
    def lower(e, mine):
        given[mine, :] = dot(hidden[mine, :], down[e], NN).astype(jnp.bfloat16)

    in_groups(0, down.shape[0], slots, lower, size=4)
    out[...] = dot(pick_back[...], given[...], NN).astype(jnp.bfloat16)


def own_kernel(slots, place, hidden, pick_back, wd, out, given, down, sems):
    share = out.shape[1]
    column = pl.multiple_of(place[1] * share, share)
    for copy in fetches((wd,), (down,), sems, column, 0):
        copy.start()

    def arrive(e):
        for copy in fetches((wd,), (down,), sems, column, 0, e):
            copy.wait()

    def lower(e, mine):
        given[mine, :] = dot(hidden[mine, :], down[e], NN).astype(jnp.bfloat16)

    in_groups(0, down.shape[0], slots, lower, None, arrive)
    out[...] = dot(pick_back[...], given[...], NN).astype(jnp.bfloat16)


def call(kernel, args, fetched, outs, scratch, micros, room):
    vmem, there = pl.BlockSpec(memory_space=pltpu.VMEM), pl.BlockSpec(memory_space=pl.ANY)
    specs = [vmem if a.ndim > 1 else pl.BlockSpec(memory_space=pltpu.SMEM) for a in args[: len(args) - fetched]]
    return pl.pallas_call(
        kernel,
        in_specs=specs + [there] * fetched,
        out_specs=jax.tree.map(lambda _: vmem, outs),
        out_shape=outs,
        scratch_shapes=scratch,
        compiler_params=pltpu.CompilerParams(vmem_limit_bytes=room << 20),
        cost_estimate=pl.CostEstimate(flops=micros * 10**9, bytes_accessed=micros * 3 * 10**6, transcendentals=0),
    )(*args)


def swap(a, axis, bits):
    n = lax.axis_size(axis)
    return lax.ppermute(a, axis, [(i, i ^ bits) for i in range(n)])


def small_group(tokens, expert_ids, route_weights, w_gate, w_up, w_down):
    steps, nrows, share = tokens.shape
    picks = expert_ids.shape[-1]
    holders = lax.axis_size("expert")
    residents = w_gate.shape[0]
    block = steps * nrows
    slots = steps * holders * CAP
    place = jnp.stack([lax.axis_index("expert") * residents, lax.axis_index("tensor")]).astype(jnp.int32)
    there = lambda a: pltpu.with_memory_space_constraint(a, pltpu.HBM)
    wg, wu, wd = there(w_gate.swapaxes(1, 2)), there(w_up.swapaxes(1, 2)), there(w_down)
    units, rows, total = wg.shape[1], holders * block, residents * slots
    shape = jax.ShapeDtypeStruct
    sources = (tokens.reshape(block, share), expert_ids.transpose(2, 0, 1), route_weights.transpose(2, 0, 1))
    mine = call(
        pack_kernel,
        tuple(there(a) for a in sources),
        3,
        shape((TILE, block // TILE * share + 2 * block), jnp.bfloat16),
        [
            pltpu.VMEM((TILE, 2 * block), jnp.float32),
            pltpu.VMEM((picks, steps, nrows), jnp.int32),
            pltpu.VMEM((picks, steps, nrows), jnp.float32),
            pltpu.SemaphoreType.DMA((2 + block // TILE,)),
        ],
        1,
        2,
    )
    sems = lambda n: pltpu.SemaphoreType.DMA((n, residents))
    several = lambda n: shape((n, units, 2 * share), jnp.bfloat16)
    scratch = lambda n: pltpu.VMEM(several(n).shape, jnp.bfloat16)
    first = residents - FIRST
    first_pair = call(early_kernel, (place, mine, wg, wu), 2, (several(first), several(first)), [sems(2)], 7, 2)
    came = {k: swap(mine, "expert", k) for k in (3, 2, 1)}
    pieces = (mine, came[1], came[2], came[3])
    pieces, first_pair = lax.optimization_barrier((pieces, first_pair))
    own = call(join_kernel, pieces, 0, shape((rows, share), jnp.bfloat16), [], 1, 2)
    core = swap(own, "tensor", 1)
    across = swap(own, "tensor", 2)
    pick_mat, pick_back = shape((total, rows), jnp.bfloat16), shape((rows, total), jnp.bfloat16)
    slot_weight, part = shape((total, 128), jnp.float32), shape((total, units), jnp.float32)
    hidden, part_out = shape((total, units), jnp.bfloat16), shape((rows, share), jnp.bfloat16)
    taken = pltpu.VMEM((total, 2 * share), jnp.bfloat16)
    pick_mat, pick_back, slot_weight, gate, up, down, *next_pair = call(
        functools.partial(half_kernel, slots),
        (place, own, core) + pieces + tuple(first_pair) + (wg, wu, wd),
        3,
        (pick_mat, pick_back, slot_weight, part, part, several(residents), several(FIRST), several(FIRST)),
        [taken, pltpu.VMEM((3 * TILE, rows), jnp.float32), scratch(FIRST), scratch(FIRST), sems(2), sems(4)],
        9,
        8,
    )
    across_late, gate = lax.optimization_barrier((across, gate))
    across_core = swap(across_late, "tensor", 1)
    given = pltpu.VMEM((total, share), jnp.bfloat16)
    narrow = pltpu.VMEM((residents, units, share), jnp.bfloat16)
    hidden, core_parts, away_down = call(
        functools.partial(rest_kernel, slots),
        (place, across, across_core, pick_mat, pick_back, slot_weight, gate, up, down, *next_pair, wg, wu, wd),
        3,
        (hidden, shape((2, rows, share), jnp.bfloat16), shape((residents, units, share), jnp.bfloat16)),
        [taken, taken, scratch(first), scratch(first), sems(2), sems(1)],
        12,
        21,
    )
    wide = lambda a: a.astype(jnp.float32)
    came_core = swap(core_parts, "tensor", 1)
    away = call(functools.partial(lower_kernel, slots), (place, hidden, pick_back, away_down), 0, part_out, [given], 3, 3)
    away = (wide(away) + wide(came_core[0])).astype(jnp.bfloat16)
    away, hidden = lax.optimization_barrier((away, hidden))
    back = swap(away, "tensor", 2)
    home = call(
        functools.partial(own_kernel, slots),
        (place, hidden, pick_back, wd),
        1,
        part_out,
        [given, narrow, sems(1)],
        4,
        8,
    )
    home = wide(home) + wide(came_core[1]) + wide(back)
    home = home.reshape(holders, block, share)
    sent = home.astype(jnp.bfloat16)
    came = {k: swap(sent[k], "expert", k) for k in (3, 2, 1)}
    result = home[0] + wide(came[1]) + wide(came[2]) + wide(came[3])
    return result.reshape(steps, nrows, share).astype(jnp.bfloat16)


def pick_plan(*arrays):
    holders, splits = lax.axis_size("expert"), lax.axis_size("tensor")
    residents = arrays[3].shape[0]
    block = arrays[0].shape[0] * arrays[0].shape[1]
    small = holders == 4 and splits == 4 and residents == 16 and block == 64
    return (small_group if small else per_device)(*arrays)


def solution(mesh):
    return jax.shard_map(
        pick_plan,
        mesh=mesh,
        in_specs=(
            P(None, ("replica", "expert"), "tensor"),
            P(None, ("replica", "expert"), None),
            P(None, ("replica", "expert"), None),
            P("expert", None, "tensor"),
            P("expert", None, "tensor"),
            P("expert", "tensor", None),
        ),
        out_specs=P(None, ("replica", "expert"), "tensor"),
        check_vma=False,
    )
```

```python
import functools

import jax
import jax.numpy as jnp
from jax import lax
from jax.experimental import pallas as pl
from jax.experimental.pallas import tpu as pltpu
from jax.sharding import PartitionSpec as P

EXPERTS = 64
CAP = 6


def slot_numbers(choice_ids):
    nblocks, nrows, npicks = choice_ids.shape
    flat_ids = choice_ids.reshape(nblocks, nrows * npicks)
    labels = lax.broadcasted_iota(jnp.int32, (1, 1, EXPERTS), 2)
    onehot = (flat_ids[:, :, None] == labels).astype(jnp.int32)
    earlier = jnp.cumsum(onehot, axis=1) - onehot
    position = jnp.sum(earlier * onehot, axis=2)
    return (flat_ids * CAP + position).reshape(nblocks, nrows, npicks)


def dispatch(slot_ids, row_data, slot_total):
    labels = lax.broadcasted_iota(jnp.int32, (1, slot_total, 1, 1), 1)
    chosen = jnp.sum((slot_ids[:, None, :, :] == labels).astype(jnp.int32), axis=3)
    placed = jnp.einsum(
        "bsr,brw->bsw", chosen.astype(jnp.bfloat16), row_data, preferred_element_type=jnp.float32
    )
    return placed.astype(jnp.bfloat16)


def expert_work(arrived_rows, w_gate, w_up, w_down):
    features = lax.all_gather(arrived_rows, "tensor", axis=3, tiled=True)
    decode_step_count, expert_holders, slot_count, feature_width = features.shape
    resident_weights = w_gate.shape[0]
    per_expert = slot_count // resident_weights
    grouped = features.reshape(
        decode_step_count, expert_holders, resident_weights, per_expert, feature_width
    )
    gate_val = jnp.einsum("bhecd,edf->bhecf", grouped, w_gate, preferred_element_type=jnp.float32)
    up_val = jnp.einsum("bhecd,edf->bhecf", grouped, w_up, preferred_element_type=jnp.float32)
    hidden = (jax.nn.silu(gate_val) * up_val).astype(jnp.bfloat16)
    partial_output_value = jnp.einsum(
        "bhecf,efd->bhecd", hidden, w_down, preferred_element_type=jnp.float32
    )
    partial_output_value = partial_output_value.astype(jnp.bfloat16)
    restored = partial_output_value.reshape(
        decode_step_count, expert_holders, slot_count, feature_width
    )
    summed = lax.psum_scatter(
        restored.astype(jnp.float32).astype(jnp.bfloat16), "tensor", scatter_dimension=3, tiled=True
    )
    return lax.all_to_all(summed, "expert", split_axis=1, concat_axis=1, tiled=True)


def per_device(tokens, expert_ids, route_weights, w_gate, w_up, w_down):
    expert_holders = lax.axis_size("expert")
    resident_weights = w_gate.shape[0]
    decode_step_count, nrows, share_width = tokens.shape
    slot_ids = slot_numbers(expert_ids)
    outgoing = dispatch(slot_ids, tokens, EXPERTS * CAP)
    outgoing = outgoing.reshape(
        decode_step_count, expert_holders, resident_weights * CAP, share_width
    )
    returned = expert_work(
        lax.all_to_all(outgoing, "expert", split_axis=1, concat_axis=1, tiled=True),
        w_gate,
        w_up,
        w_down,
    )
    returned = returned.reshape(decode_step_count, EXPERTS * CAP, share_width)
    labels = lax.broadcasted_iota(jnp.int32, (1, 1, 1, EXPERTS * CAP), 3)
    selector = (slot_ids[..., None] == labels).astype(jnp.bfloat16)
    picked = jnp.einsum("brks,bsw->brkw", selector, returned, preferred_element_type=jnp.float32)
    combined = jnp.sum(picked * route_weights[..., None], axis=2)
    return combined.astype(jnp.bfloat16)


NT = (((1,), (1,)), ((), ()))
NN = (((1,), (0,)), ((), ()))
TN = (((0,), (0,)), ((), ()))
TILE = 16
TOPK = 6
GROUP = 4
FIRST = 4


def dot(a, b, dims):
    return lax.dot_general(a, b, dims, preferred_element_type=jnp.float32)


def pack_kernel(tokens, ids_there, weights_there, out, table, ids, weights, sems):
    share = tokens.shape[1]
    wide = out.shape[1] - table.shape[1]
    copies = [
        pltpu.make_async_copy(ids_there, ids, sems.at[0]),
        pltpu.make_async_copy(weights_there, weights, sems.at[1]),
    ]
    for j in range(wide // share):
        tile = tokens.at[j * TILE : (j + 1) * TILE]
        copies.append(pltpu.make_async_copy(tile, out.at[:, j * share : (j + 1) * share], sems.at[2 + j]))
    for copy in copies:
        copy.start()
    table[...] = jnp.zeros_like(table)
    wait_all(copies[:2])
    picks, steps, step_rows = ids.shape
    half = steps * step_rows
    for s in range(steps):
        high = weights[:, s, :].astype(jnp.bfloat16).astype(jnp.float32)
        low = weights[:, s, :] - high
        at = s * step_rows
        table[:picks, at : at + step_rows] = ids[:, s, :].astype(jnp.float32)
        table[8 : 8 + picks, at : at + step_rows] = high
        table[:picks, half + at : half + at + step_rows] = low
    out[:, wide:] = table[...].astype(jnp.bfloat16)
    wait_all(copies[2:])


def early_kernel(place, packed, wg, wu, first_g, first_u, sems):
    copies = fetches((wg, wu), (first_g, first_u), sems, near_pair(place, first_g), 0)
    for copy in copies:
        copy.start()
    for copy in copies:
        copy.wait()


def join_kernel(first, second, third, fourth, out):
    share = out.shape[1]
    block = out.shape[0] // 4
    for i, piece in enumerate((first, second, third, fourth)):
        for j in range(block // TILE):
            out[i * block + j * TILE : i * block + (j + 1) * TILE, :] = piece[:, j * share : (j + 1) * share]


def route(place, pieces, picks, slots, residents, table, pick_mat, slot_weight):
    rows = table.shape[1]
    block = rows // len(pieces)
    for j, piece in enumerate(pieces):
        packed = piece[:, piece.shape[1] - 2 * block :].astype(jnp.float32)
        here = slice(j * block, (j + 1) * block)
        table[:8, here] = packed[:8, :block]
        table[TILE : TILE + 8, here] = packed[8:, :block]
        table[2 * TILE : 2 * TILE + 8, here] = packed[:8, block:]
    labels = (place[0] + lax.broadcasted_iota(jnp.int32, (residents, rows), 0)).astype(jnp.float32)
    chosen = jnp.zeros((residents, rows), jnp.float32)
    weight = jnp.zeros((residents, rows), jnp.float32)
    for k in range(picks):
        hit = table[k : k + 1, :] == labels
        share = table[TILE + k : TILE + k + 1, :] + table[2 * TILE + k : 2 * TILE + k + 1, :]
        chosen = jnp.where(hit, 1.0, chosen)
        weight = jnp.where(hit, share, weight)
    before = lax.broadcasted_iota(jnp.int32, (rows, rows), 0) < lax.broadcasted_iota(jnp.int32, (rows, rows), 1)
    rank = dot(chosen.astype(jnp.bfloat16), before.astype(jnp.bfloat16), NN)
    rank = jnp.where(chosen > 0.0, rank, -1.0)
    numbers = lax.broadcasted_iota(jnp.int32, (slots, rows), 0).astype(jnp.float32)
    for e in range(residents):
        hit = numbers == rank[e : e + 1, :]
        pick_mat[e * slots : (e + 1) * slots, :] = hit.astype(jnp.bfloat16)
        spread = jnp.sum(jnp.where(hit, weight[e : e + 1, :], 0.0), axis=1, keepdims=True)
        slot_weight[e * slots : (e + 1) * slots, :] = jnp.broadcast_to(spread, (slots, 128))


def near_pair(place, buffer):
    width = buffer.shape[2]
    return pl.multiple_of((place[1] >> 1) * width, width)


def far_pair(place, buffer):
    width = buffer.shape[2]
    return pl.multiple_of(((place[1] >> 1) ^ 1) * width, width)


def fetches(weights, buffers, sems, column, first, one=None):
    count, _, width = buffers[0].shape
    return [
        pltpu.make_async_copy(w.at[first + e, :, pl.ds(column, width)], b.at[e], sems.at[i, e])
        for e in (range(count) if one is None else (one,))
        for i, (w, b) in enumerate(zip(weights, buffers))
    ]


def wait_all(copies):
    for copy in copies:
        copy.wait()


def place_rows(place, pick_mat, near, far, taken):
    share = near.shape[1]
    low = place[1] & 1
    for column, piece in ((low, near), (1 - low, far)):
        rows = dot(pick_mat[...], piece[...], NN).astype(jnp.bfloat16)
        taken[:, pl.ds(pl.multiple_of(column * share, share), share)] = rows


def in_groups(first, last, slots, work, after=None, arrive=None, size=2):
    def some(step, carry):
        group = [first + step * size + g for g in range(size)]
        places = [pl.ds(pl.multiple_of(e * slots, slots), slots) for e in group]
        for e in group if arrive else ():
            arrive(e)
        for e, mine in zip(group, places):
            work(e, mine)
        for e, mine in zip(group, places) if after else ():
            after(e, mine)
        return carry

    lax.fori_loop(0, (last - first) // size, some, 0)


def half_kernel(slots, place, near, far, one, two, three, four, first_g, first_u, wg, wu, wd, *rest):
    pick_mat, pick_back, slot_weight, gate, up, down, next_g, next_u, taken, table, bg, bu, sems, ahead = rest
    held = first_g.shape[0]
    residents = held + bg.shape[0]
    later = far_pair(place, bg)
    copies = fetches((wg, wu), (bg, bu), sems, near_pair(place, bg), held)
    share = near.shape[1]
    early = [
        pltpu.make_async_copy(
            wd.at[e, :, pl.ds(pl.multiple_of((place[1] ^ (3 - 2 * j)) * share, share), share)],
            down.at[e, :, j * share : (j + 1) * share],
            ahead.at[2 + j, e],
        )
        for e in range(residents)
        for j in range(2)
    ]
    early = early + fetches((wg, wu), (next_g, next_u), ahead, later, 0)
    for copy in copies + early:
        copy.start()
    route(place, (one, two, three, four), TOPK, slots, residents, table, pick_mat, slot_weight)
    place_rows(place, pick_mat, near, far, taken)
    pick_back[...] = pick_mat[...].T

    def work(e, mine, g_block, u_block):
        x = taken[mine, :]
        gate[mine, :] = dot(x, g_block, NT)
        up[mine, :] = dot(x, u_block, NT)

    in_groups(0, held, slots, lambda e, mine: work(e, mine, first_g[e], first_u[e]), size=3)
    wait_all(copies)
    in_groups(held, residents, slots, lambda e, mine: work(e, mine, bg[e - held], bu[e - held]), size=GROUP)
    wait_all(early)


def rest_kernel(slots, place, near, far, pick_mat, pick_back, slot_weight, gate, up, down, next_g, next_u, *rest):
    wg, wu, wd, hidden, out, away_down, taken, given, bg, bu, sems, ahead = rest
    held = next_g.shape[0]
    residents = held + bg.shape[0]
    share = out.shape[2]
    away_columns = pl.multiple_of((place[1] ^ 2) * share, share)
    early = fetches((wd,), (away_down,), ahead, away_columns, 0)
    for copy in fetches((wg, wu), (bg, bu), sems, far_pair(place, bg), held) + early:
        copy.start()
    place_rows(place, pick_mat, near, far, taken)

    def work(e, mine, g_block, u_block):
        x = taken[mine, :]
        gate_val = gate[mine, :] + dot(x, g_block, NT)
        up_val = up[mine, :] + dot(x, u_block, NT)
        scaled = gate_val * jax.nn.sigmoid(gate_val) * up_val * slot_weight[mine, :1]
        hidden[mine, :] = scaled.astype(jnp.bfloat16)

    def lower(e, mine):
        given[mine, :] = dot(hidden[mine, :], down[e], NN).astype(jnp.bfloat16)

    def arrive(e):
        wait_all(fetches((wg, wu), (bg, bu), sems, far_pair(place, bg), held, e - held))

    in_groups(0, held, slots, lambda e, mine: work(e, mine, next_g[e], next_u[e]), lower)
    in_groups(held, residents, slots, lambda e, mine: work(e, mine, bg[e - held], bu[e - held]), lower, arrive, 3)
    wait_all(early)
    for j in range(2):
        out[j] = dot(pick_back[...], given[:, j * share : (j + 1) * share], NN).astype(jnp.bfloat16)


def lower_kernel(slots, place, hidden, pick_back, down, out, given):
    def lower(e, mine):
        given[mine, :] = dot(hidden[mine, :], down[e], NN).astype(jnp.bfloat16)

    in_groups(0, down.shape[0], slots, lower, size=8)
    out[...] = dot(pick_back[...], given[...], NN).astype(jnp.bfloat16)


def own_kernel(slots, place, hidden, pick_back, wd, out, given, down, sems):
    share = out.shape[1]
    column = pl.multiple_of(place[1] * share, share)
    for copy in fetches((wd,), (down,), sems, column, 0):
        copy.start()

    def arrive(e):
        for copy in fetches((wd,), (down,), sems, column, 0, e):
            copy.wait()

    def lower(e, mine):
        given[mine, :] = dot(hidden[mine, :], down[e], NN).astype(jnp.bfloat16)

    in_groups(0, down.shape[0], slots, lower, None, arrive)
    out[...] = dot(pick_back[...], given[...], NN).astype(jnp.bfloat16)


def call(kernel, args, fetched, outs, scratch, micros, room):
    vmem, there = pl.BlockSpec(memory_space=pltpu.VMEM), pl.BlockSpec(memory_space=pl.ANY)
    specs = [vmem if a.ndim > 1 else pl.BlockSpec(memory_space=pltpu.SMEM) for a in args[: len(args) - fetched]]
    return pl.pallas_call(
        kernel,
        in_specs=specs + [there] * fetched,
        out_specs=jax.tree.map(lambda _: vmem, outs),
        out_shape=outs,
        scratch_shapes=scratch,
        compiler_params=pltpu.CompilerParams(vmem_limit_bytes=room << 20),
        cost_estimate=pl.CostEstimate(flops=micros * 10**9, bytes_accessed=micros * 3 * 10**6, transcendentals=0),
    )(*args)


def swap(a, axis, bits):
    n = lax.axis_size(axis)
    return lax.ppermute(a, axis, [(i, i ^ bits) for i in range(n)])


def small_group(tokens, expert_ids, route_weights, w_gate, w_up, w_down):
    steps, nrows, share = tokens.shape
    picks = expert_ids.shape[-1]
    holders = lax.axis_size("expert")
    residents = w_gate.shape[0]
    block = steps * nrows
    slots = steps * holders * CAP
    place = jnp.stack([lax.axis_index("expert") * residents, lax.axis_index("tensor")]).astype(jnp.int32)
    there = lambda a: pltpu.with_memory_space_constraint(a, pltpu.HBM)
    wg, wu, wd = there(w_gate.swapaxes(1, 2)), there(w_up.swapaxes(1, 2)), there(w_down)
    units, rows, total = wg.shape[1], holders * block, residents * slots
    shape = jax.ShapeDtypeStruct
    sources = (tokens.reshape(block, share), expert_ids.transpose(2, 0, 1), route_weights.transpose(2, 0, 1))
    mine = call(
        pack_kernel,
        tuple(there(a) for a in sources),
        3,
        shape((TILE, block // TILE * share + 2 * block), jnp.bfloat16),
        [
            pltpu.VMEM((TILE, 2 * block), jnp.float32),
            pltpu.VMEM((picks, steps, nrows), jnp.int32),
            pltpu.VMEM((picks, steps, nrows), jnp.float32),
            pltpu.SemaphoreType.DMA((2 + block // TILE,)),
        ],
        1,
        2,
    )
    sems = lambda n: pltpu.SemaphoreType.DMA((n, residents))
    several = lambda n: shape((n, units, 2 * share), jnp.bfloat16)
    scratch = lambda n: pltpu.VMEM(several(n).shape, jnp.bfloat16)
    first = residents - FIRST
    first_pair = call(early_kernel, (place, mine, wg, wu), 2, (several(first), several(first)), [sems(2)], 7, 2)
    came = {k: swap(mine, "expert", k) for k in (3, 2, 1)}
    pieces = (mine, came[1], came[2], came[3])
    pieces, first_pair = lax.optimization_barrier((pieces, first_pair))
    own = call(join_kernel, pieces, 0, shape((rows, share), jnp.bfloat16), [], 1, 2)
    core = swap(own, "tensor", 1)
    across = swap(own, "tensor", 2)
    pick_mat, pick_back = shape((total, rows), jnp.bfloat16), shape((rows, total), jnp.bfloat16)
    slot_weight, part = shape((total, 128), jnp.float32), shape((total, units), jnp.float32)
    hidden, part_out = shape((total, units), jnp.bfloat16), shape((rows, share), jnp.bfloat16)
    taken = pltpu.VMEM((total, 2 * share), jnp.bfloat16)
    pick_mat, pick_back, slot_weight, gate, up, down, *next_pair = call(
        functools.partial(half_kernel, slots),
        (place, own, core) + pieces + tuple(first_pair) + (wg, wu, wd),
        3,
        (pick_mat, pick_back, slot_weight, part, part, several(residents), several(FIRST), several(FIRST)),
        [taken, pltpu.VMEM((3 * TILE, rows), jnp.float32), scratch(FIRST), scratch(FIRST), sems(2), sems(4)],
        9,
        8,
    )
    across_late, gate = lax.optimization_barrier((across, gate))
    across_core = swap(across_late, "tensor", 1)
    given = pltpu.VMEM((total, share), jnp.bfloat16)
    narrow = pltpu.VMEM((residents, units, share), jnp.bfloat16)
    hidden, core_parts, away_down = call(
        functools.partial(rest_kernel, slots),
        (place, across, across_core, pick_mat, pick_back, slot_weight, gate, up, down, *next_pair, wg, wu, wd),
        3,
        (hidden, shape((2, rows, share), jnp.bfloat16), shape((residents, units, share), jnp.bfloat16)),
        [taken, taken, scratch(first), scratch(first), sems(2), sems(1)],
        12,
        21,
    )
    wide = lambda a: a.astype(jnp.float32)
    came_core = swap(core_parts, "tensor", 1)
    away = call(functools.partial(lower_kernel, slots), (place, hidden, pick_back, away_down), 0, part_out, [given], 3, 3)
    away = (wide(away) + wide(came_core[0])).astype(jnp.bfloat16)
    away, hidden = lax.optimization_barrier((away, hidden))
    back = swap(away, "tensor", 2)
    home = call(
        functools.partial(own_kernel, slots),
        (place, hidden, pick_back, wd),
        1,
        part_out,
        [given, narrow, sems(1)],
        4,
        8,
    )
    home = wide(home) + wide(came_core[1]) + wide(back)
    home = home.reshape(holders, block, share)
    sent = home.astype(jnp.bfloat16)
    came = {k: swap(sent[k], "expert", k) for k in (3, 2, 1)}
    result = home[0] + wide(came[1]) + wide(came[2]) + wide(came[3])
    return result.reshape(steps, nrows, share).astype(jnp.bfloat16)


def pick_plan(*arrays):
    holders, splits = lax.axis_size("expert"), lax.axis_size("tensor")
    residents = arrays[3].shape[0]
    block = arrays[0].shape[0] * arrays[0].shape[1]
    small = holders == 4 and splits == 4 and residents == 16 and block == 64
    return (small_group if small else per_device)(*arrays)


def solution(mesh):
    return jax.shard_map(
        pick_plan,
        mesh=mesh,
        in_specs=(
            P(None, ("replica", "expert"), "tensor"),
            P(None, ("replica", "expert"), None),
            P(None, ("replica", "expert"), None),
            P("expert", None, "tensor"),
            P("expert", None, "tensor"),
            P("expert", "tensor", None),
        ),
        out_specs=P(None, ("replica", "expert"), "tensor"),
        check_vma=False,
    )
```
